256 devices in a mesh: lon: 64 (over z, y, x_lo), lat: 4 (over x_hi, core).
Axes of the slice: x: 4 (x_hi: 2, x_lo: 2; x = x_hi * 2 + x_lo), y: 4, z: 8, core: 2. Of those that a mesh axis runs over, the one named last changes fastest.
Arguments:
- thermal_anomaly: float32 [3, 1024, 8192], P(None, 'lat', 'lon'), may hold values from -6 to 6
- saltiness_anomaly: float32 [3, 1024, 8192], P(None, 'lat', 'lon'), may hold values from -6 to 6
- zonal_transport_ratio: float32 [3, 1024, 8192], P(None, 'lat', 'lon'), may hold values from -0.15 to 0.15
- meridional_transport_ratio: float32 [3, 1024, 8192], P(None, 'lat', 'lon'), may hold values from -0.15 to 0.15
- mixing_factor: float32 [3, 1024, 8192], P(None, 'lat', 'lon'), may hold values from 0.01 to 0.08
- water_indicator: int32 [3, 1024, 8192], P(None, 'lat', 'lon'), may hold values 0 or 1
- seam_mirror_index: int32 [8192], P('lon'), may hold values from 0 to 8191, as said below
Outputs:
- new_temperature: float32 [3, 1024, 8192], P(None, 'lat', 'lon')
- new_salinity: float32 [3, 1024, 8192], P(None, 'lat', 'lon')
- density: float32 [3, 1024, 8192], P(None, 'lat', 'lon')
The draws below stay inside these ranges and needn't reach their ends.
Inputs may be any that keep to these rules, and one draw needn't show every extreme that they name: `seam_mirror_index`: the columns are in blocks of 128; every column of block d meets a column of block (r - 1 - d) modulo 8192 / 128, with one whole number r drawn from the seed, and the columns of one block meet the columns of their partner block each exactly once.
All inputs are finite; a program needn't handle non-finite values. No bound on the sum of `water_indicator` on one device may be relied on, other than what follows from the above.
Results may differ from the reference program's by a relative error of at most 0.00002.
Values sent between devices are 32-bit elements; how exact they have to be, the bound alone decides.
No kernel may reach another device: no remote copies, remote signals or barrier semaphores. Data moves between devices by JAX's collectives and lax.ppermute only.
A program may use at most 192 MiB of HBM per device.

```python
import math
import jax
import jax.numpy as jnp

CX = 128
LAYER_TOTAL = 3
STEPS = 4
PARALLEL_CELLS = 8192
MERIDIAN_ROWS = 1024


def draw_seam_mirror_index(key, part):
    key = jax.random.fold_in(key, 11)
    block_count = PARALLEL_CELLS // CX
    rotation = jax.random.randint(jax.random.fold_in(key, 1), (), 0, block_count)
    block_keys = jax.random.split(jax.random.fold_in(key, 2), block_count)
    orders = jax.vmap(lambda one_key: jax.random.permutation(one_key, CX))(block_keys).astype(jnp.int32)
    blocks = jnp.arange(block_count, dtype=jnp.int32)
    partner_block = jnp.mod(rotation - 1 - blocks, block_count).astype(jnp.int32)
    columns = partner_block[:, None] * CX + orders
    return columns.reshape(PARALLEL_CELLS).astype(jnp.int32)


def plant(result, key, low, high):
    longest = result.shape.index(max(result.shape))
    spots = []
    for shift in (0, 1):
        where = [jax.random.randint(jax.random.fold_in(key, axis), (), 0, length) for axis, length in enumerate(result.shape)]
        where[longest] = (where[longest] + shift) % result.shape[longest]
        spots.append(tuple(where))
    return result.at[spots[0]].set(low).at[spots[1]].set(high)


def shard_levels(rng, dims, cuts, least, high):
    level = 1.0
    for position, blocks in cuts:
        steps = jax.random.uniform(jax.random.fold_in(jax.random.fold_in(rng, 6), position), (blocks,), jnp.float32, least / len(cuts), high / len(cuts))
        level = level * jnp.repeat(jnp.exp(steps), dims[position] // blocks).reshape((-1,) + (1,) * (len(dims) - 1 - position))
    return level


def bell_draw(rng, extent, spread, reach, cuts=(), kind=jnp.bfloat16):
    result = jax.random.normal(rng, extent, jnp.float32) * spread
    if len(cuts) > 0:
        result = shard_levels(rng, extent, cuts, -0.22, 0.18) * result
    return jnp.clip(result, min=-reach, max=reach).astype(kind)


def setup_inputs(seed: int = 0) -> dict:
    key_of = jax.random.split(jax.random.key(seed), 8)
    thermal_anomaly = bell_draw(key_of[0], (LAYER_TOTAL, MERIDIAN_ROWS, PARALLEL_CELLS), 1.0, 6.0, ((1, 4), (2, 64)), jnp.float32)
    saltiness_anomaly = bell_draw(key_of[1], (LAYER_TOTAL, MERIDIAN_ROWS, PARALLEL_CELLS), 1.0, 6.0, ((1, 4), (2, 64)), jnp.float32)
    zonal_transport_ratio = jnp.clip(jax.random.uniform(key_of[2], (LAYER_TOTAL, MERIDIAN_ROWS, PARALLEL_CELLS), jnp.float32, -0.15, 0.15) * shard_levels(key_of[2], (LAYER_TOTAL, MERIDIAN_ROWS, PARALLEL_CELLS), ((1, 4), (2, 64)), -0.4, 0.0), -0.15, 0.15)
    meridional_transport_ratio = jnp.clip(jax.random.uniform(key_of[3], (LAYER_TOTAL, MERIDIAN_ROWS, PARALLEL_CELLS), jnp.float32, -0.15, 0.15) * shard_levels(key_of[3], (LAYER_TOTAL, MERIDIAN_ROWS, PARALLEL_CELLS), ((1, 4), (2, 64)), -0.4, 0.0), -0.15, 0.15)
    mixing_factor = jnp.clip(jnp.exp(math.log(0.08) - 2.0794415 * jax.random.uniform(key_of[4], (LAYER_TOTAL, MERIDIAN_ROWS, PARALLEL_CELLS), jnp.float32) ** shard_levels(key_of[4], (LAYER_TOTAL, MERIDIAN_ROWS, PARALLEL_CELLS), ((1, 4), (2, 64)), -0.2, 0.2)), 0.01, 0.08)
    water_indicator = plant((jax.random.randint(key_of[5], (LAYER_TOTAL, MERIDIAN_ROWS, PARALLEL_CELLS), 0, 4) < 3).astype(jnp.int32), jax.random.fold_in(key_of[5], 1), 0, 1)
    seam_mirror_index = draw_seam_mirror_index(jax.random.fold_in(key_of[7], 71), 0)
    return {"thermal_anomaly": thermal_anomaly, "saltiness_anomaly": saltiness_anomaly, "zonal_transport_ratio": zonal_transport_ratio, "meridional_transport_ratio": meridional_transport_ratio, "mixing_factor": mixing_factor, "water_indicator": water_indicator, "seam_mirror_index": seam_mirror_index}


def neighbours(field, partner):
    westward = jnp.roll(field, 1, axis=-1)
    eastward = jnp.roll(field, -1, axis=-1)
    zero_row = jnp.zeros_like(field[..., :1, :])
    southward = jnp.concatenate([zero_row, field[..., :-1, :]], axis=-2)
    ghost_row = jnp.take(field[..., MERIDIAN_ROWS - 2, :], partner, axis=-1)
    northward = jnp.concatenate([field[..., 1:, :], ghost_row[..., None, :]], axis=-2)
    return westward, eastward, southward, northward


def face_flux(lower, upper, speed, opened, coeff):
    return opened * (jnp.maximum(speed, 0.0) * lower + jnp.minimum(speed, 0.0) * upper - coeff * (upper - lower))


def advance(scalar_quantities, sides, sea, faces):
    open_w, open_e, open_s, open_n, dif_w, dif_e, dif_s, dif_n, speed_e, speed_w, speed_n, speed_s = faces
    westward, eastward, southward, northward = sides
    east_flux = face_flux(scalar_quantities, eastward, speed_e, open_e, dif_e)
    west_flux = face_flux(westward, scalar_quantities, speed_w, open_w, dif_w)
    north_flux = face_flux(scalar_quantities, northward, speed_n, open_n, dif_n)
    south_flux = face_flux(southward, scalar_quantities, speed_s, open_s, dif_s)
    return sea * (scalar_quantities - (east_flux - west_flux) - (north_flux - south_flux))


def reference(thermal_anomaly, saltiness_anomaly, zonal_transport_ratio, meridional_transport_ratio, mixing_factor, water_indicator, seam_mirror_index):
    sea = water_indicator.astype(jnp.float32)
    sea_w, sea_e, sea_s, sea_n = neighbours(sea, seam_mirror_index)
    kap_w, kap_e, kap_s, kap_n = neighbours(mixing_factor, seam_mirror_index)
    speed_w = jnp.roll(zonal_transport_ratio, 1, axis=-1)
    speed_s = jnp.concatenate([jnp.zeros_like(meridional_transport_ratio[:, :1, :]), meridional_transport_ratio[:, :-1, :]], axis=1)
    faces = (sea_w * sea, sea * sea_e, sea_s * sea, sea * sea_n,
             0.5 * (kap_w + mixing_factor), 0.5 * (mixing_factor + kap_e),
             0.5 * (kap_s + mixing_factor), 0.5 * (mixing_factor + kap_n),
             zonal_transport_ratio, speed_w, meridional_transport_ratio, speed_s)
    scalar_quantities = jnp.stack([thermal_anomaly, saltiness_anomaly])
    for step in range(STEPS):
        scalar_quantities = advance(scalar_quantities, neighbours(scalar_quantities, seam_mirror_index), sea, faces)
    heat = scalar_quantities[0]
    salt_new = scalar_quantities[1]
    density = sea * (-0.2 * heat * (1.0 + 0.05 * heat) + 0.8 * salt_new - 0.01 * heat * salt_new)
    return heat, salt_new, density
```

```python
import functools

import jax
import jax.numpy as jnp
from jax import lax
from jax.experimental import pallas as pl
from jax.experimental.pallas import tpu as pltpu
from jax.sharding import PartitionSpec as P

STEPS = 4
LEVELS = 3
ROWS = 256
COLS = 128
LON = 64
LAT = 4
AXES = ("lon", "lat")
HALF = LON // 2

BASE = 16
NORTH = BASE + ROWS
EXT = 288
FIRST_BLOCK = 8
BLOCKS = 34

TILES = 23


def flat(lon, lat):
    return (lon % LON) * LAT + lat


def lon_pairs(partner):
    return [(flat(i, a), flat(partner(i), a)) for i in range(LON) for a in range(LAT)]


PAIR_X = lon_pairs(lambda i: i ^ 1)
PAIR_Y = lon_pairs(lambda i: ((i - 1) ^ 1) + 1)
PAIR_A = [(flat(i, a), flat(i, a ^ 1)) for i in range(LON) for a in range(LAT)]
PAIR_B = [(flat(i, a), flat(i, 3 - a)) for i in range(LON) for a in (1, 2)]


def fold_pairs(r):
    top = [(flat(i, 3), flat(r - 1 - i, 3)) for i in range(LON)]
    relay = [(flat(i, 2), flat(r + HALF - 1 - i, 2)) for i in range(LON)]
    return top + relay


def swap(x, pairs):
    return lax.ppermute(x, AXES, pairs)


def iota(axis):
    return lax.broadcasted_iota(jnp.int32, (8, COLS), axis)


def roll(x, shift, axis=1):
    return pltpu.roll(x, shift % x.shape[axis], axis)


def sea_of(x):
    return x.astype(jnp.float32)


def vmem(n):
    return [pl.BlockSpec(memory_space=pltpu.VMEM)] * n


def whole(rows):
    return pl.BlockSpec((rows, COLS), lambda i: (0, 0))


PARAMS = pltpu.CompilerParams(vmem_limit_bytes=48 << 20)


def pack_kernel(t_ref, s_ref, u_ref, v_ref, k_ref, w_ref, m_ref, xs_ref, ys_ref, pt_ref, pc_ref):
    odd = lax.rem(lax.axis_index("lon"), 2) == 1
    lane = iota(1)
    group = lane >> 3
    low = (lane & 7) < 4

    def block(i, carry):
        rows = pl.ds(pl.multiple_of(i * 8, 8), 8)
        tracers = jnp.zeros((8, COLS), jnp.float32)
        for t, ref in enumerate((t_ref, s_ref)):
            for l in range(LEVELS):
                j = 3 * t + l
                tracers = jnp.where(group == j, roll(ref[l, rows, :], 4 + 8 * j), tracers)
        coefs = jnp.zeros((8, COLS), jnp.float32)
        for f, ref in enumerate((u_ref, v_ref, k_ref, w_ref)):
            for l in range(LEVELS):
                j = 3 * f + l
                x = ref[l, rows, :]
                if f == 3:
                    x = sea_of(x)
                coefs = jnp.where(group == j, roll(x, 4 + 8 * j), coefs)
        pt_ref[rows, :] = tracers
        pc_ref[rows, :] = coefs
        east = jnp.where(low, coefs, roll(tracers, 4))
        west = jnp.where(low, roll(tracers, -4), coefs)
        xs_ref[rows, :] = jnp.where(odd, west, east)
        ys_ref[rows, :] = jnp.where(odd, east, west)
        return carry

    lax.fori_loop(0, ROWS // 8, block, 0, unroll=4)
    second = ROWS - 2
    for out in (xs_ref, ys_ref):
        for l in range(LEVELS):
            one = slice(second, second + 1)
            out[pl.ds(256 + l, 1), :] = t_ref[l, one, :]
            out[pl.ds(259 + l, 1), :] = s_ref[l, one, :]
            out[pl.ds(262 + l, 1), :] = sea_of(w_ref[l, one, :])
            out[pl.ds(265 + l, 1), :] = k_ref[l, one, :]
        out[pl.ds(268, 1), :] = m_ref[...].astype(jnp.float32)
        out[pl.ds(269, 3), :] = jnp.zeros((3, COLS), jnp.float32)


def pack(t, s, u, v, k, w, m):
    edge = jax.ShapeDtypeStruct((ROWS + 16, COLS), jnp.float32)
    own = jax.ShapeDtypeStruct((ROWS, COLS), jnp.float32)
    return pl.pallas_call(
        pack_kernel,
        out_shape=(edge, edge, own, own),
        in_specs=vmem(7),
        out_specs=tuple(vmem(4)),
        compiler_params=PARAMS,
        name="pack",
    )(t, s, u, v, k, w, m)


def strips(pt, pc, mw, me):
    lane = iota(1)
    low = (lane & 7) < 4
    wt = jnp.where(low, roll(mw, -4), pt)
    et = jnp.where(low, pt, roll(me, 4))
    wc = jnp.where(low, mw, pc)
    ec = jnp.where(low, pc, me)
    out = [jnp.where(lane < 48, wt, roll(et, 48))]
    for f in range(4):
        west = jnp.where(lane < 24, roll(wc, -24 * f), roll(wc, 24 - 24 * f))
        east = jnp.where(lane < 72, roll(ec, 48 - 24 * f), roll(ec, 72 - 24 * f))
        out.append(jnp.where(lane < 48, west, east))
    return out


def rows_kernel(*refs):
    south = refs[0:6]
    north = refs[6:12]
    pts, ptn, pcs, pcn, xrs, xrn, yrs, yrn, xre, yre, m_ref = refs[12:23]
    a_ref, b_ref, f_ref = refs[23:26]
    odd = lax.rem(lax.axis_index("lon"), 2) == 1
    odd_lat = lax.rem(lax.axis_index("lat"), 2) == 1

    def tiles(fields, pt, pc, xr, yr):
        x, y = xr[...], yr[...]
        mw, me = jnp.where(odd, x, y), jnp.where(odd, y, x)
        out = []
        for f, ref in enumerate(fields):
            for l in range(LEVELS):
                x = ref[l]
                out.append(sea_of(x) if f == 5 else x)
        return out + strips(pt[...], pc[...], mw, me)

    top = tiles(north, ptn, pcn, xrn, yrn)
    bottom = tiles(south, pts, pcs, xrs, yrs)
    for j in range(TILES):
        f_ref[pl.ds(8 * j, 8), :] = top[j]
        up, down = top[j][4:8, :], bottom[j][0:4, :]
        a_ref[pl.ds(4 * j, 4), :] = jnp.where(odd_lat, down, up)
        b_ref[pl.ds(4 * j, 4), :] = jnp.where(odd_lat, up, down)
    a_ref[pl.ds(4 * TILES, 4), :] = jnp.zeros((4, COLS), jnp.float32)
    b_ref[pl.ds(4 * TILES, 4), :] = jnp.zeros((4, COLS), jnp.float32)
    x, y = xre[...], yre[...]
    ew, ee = jnp.where(odd, x, y), jnp.where(odd, y, x)
    row = iota(0)
    own = jnp.broadcast_to(m_ref[...].astype(jnp.float32), (8, COLS))
    west = jnp.broadcast_to(ew[4:5, :], (8, COLS))
    east = jnp.broadcast_to(ee[4:5, :], (8, COLS))
    f_ref[pl.ds(8 * TILES, 8), :] = jnp.where(row == 0, own, jnp.where(row == 1, west, east))


def rows(fields, pt, pc, xr, yr, m):
    last = ROWS // 8 - 1
    low3 = pl.BlockSpec((LEVELS, 8, COLS), lambda i: (0, 0, 0))
    top3 = pl.BlockSpec((LEVELS, 8, COLS), lambda i: (0, last, 0))
    low = pl.BlockSpec((8, COLS), lambda i: (0, 0))
    top = pl.BlockSpec((8, COLS), lambda i: (last, 0))
    extra = pl.BlockSpec((8, COLS), lambda i: (last + 2, 0))
    msg = jax.ShapeDtypeStruct((4 * TILES + 4, COLS), jnp.float32)
    return pl.pallas_call(
        rows_kernel,
        out_shape=(msg, msg, jax.ShapeDtypeStruct((8 * TILES + 8, COLS), jnp.float32)),
        grid=(1,),
        in_specs=[low3] * 6
        + [top3] * 6
        + [low, top] * 4
        + [extra, extra, pl.BlockSpec((1, COLS), lambda i: (0, 0))],
        out_specs=(whole(4 * TILES + 4), whole(4 * TILES + 4), whole(8 * TILES + 8)),
        compiler_params=PARAMS,
        name="rows",
    )(*fields, *fields, pt, pt, pc, pc, xr, xr, yr, yr, xr, yr, m)


def coefficients(k, s, u, v, kn, ke, ks, kw, sn, se, ss, sw, uw, vs):
    zero = jnp.zeros_like(k)
    fe, fw, fn, fs = 0.5 * (k + ke), 0.5 * (kw + k), 0.5 * (k + kn), 0.5 * (ks + k)
    oe, ow, on, os = s * se, sw * s, s * sn, ss * s
    ae, be = oe * (jnp.maximum(u, zero) + fe), oe * (jnp.minimum(u, zero) - fe)
    aw, bw = ow * (jnp.maximum(uw, zero) + fw), ow * (jnp.minimum(uw, zero) - fw)
    an, bn = on * (jnp.maximum(v, zero) + fn), on * (jnp.minimum(v, zero) - fn)
    a_s, bs = os * (jnp.maximum(vs, zero) + fs), os * (jnp.minimum(vs, zero) - fs)
    centre = s - (ae - bw) - (an - bs)
    return centre, -be, aw, -bn, a_s


def stencil(c, q, e, w, n, s):
    return c[0] * q + c[1] * e + c[2] * w + c[3] * n + c[4] * s


def edges(strip):
    return jnp.where((iota(1) & 7) == 3, strip, roll(strip, -50))


def beside(x, edge, j):
    lane = iota(1)
    z = roll(edge, -(8 * j + 3))
    return jnp.where(lane == COLS - 1, z, roll(x, -1)), jnp.where(lane == 0, z, roll(x, 1))


def gather(x, index):
    return jnp.take_along_axis(x, index, axis=1)


def ghost_kernel(p_ref, d_ref, xe_ref, ye_ref, g_ref):
    odd = lax.rem(lax.axis_index("lon"), 2) == 1
    row, lane = iota(0), iota(1)
    top = row == 7

    def tile(ref, j):
        return ref[pl.ds(8 * j, 8), :]

    def spread(index_row):
        return jnp.broadcast_to(index_row.astype(jnp.int32) & (COLS - 1), (8, COLS))

    index_d = spread(d_ref[pl.ds(8 * TILES, 1), :])
    index_p = spread(p_ref[pl.ds(8 * TILES, 1), :])
    index_pw = spread(p_ref[pl.ds(8 * TILES + 1, 1), :])
    index_pe = spread(p_ref[pl.ds(8 * TILES + 2, 1), :])
    xe0, ye0 = xe_ref[pl.ds(0, 8), :], ye_ref[pl.ds(0, 8), :]
    xe1, ye1 = xe_ref[pl.ds(8, 8), :], ye_ref[pl.ds(8, 8), :]
    east = [gather(jnp.where(odd, y, x), index_pw) for x, y in ((xe0, ye0), (xe1, ye1))]
    west = [gather(jnp.where(odd, x, y), index_pe) for x, y in ((xe0, ye0), (xe1, ye1))]

    def outer(kind):
        out = jnp.zeros((8, COLS), jnp.float32)
        for j in range(6):
            n = (j, 6 + j % 3, 9 + j % 3)[kind]
            w = jnp.broadcast_to(east[n // 8][n % 8 : n % 8 + 1, :], (8, COLS))
            e = jnp.broadcast_to(west[n // 8][n % 8 : n % 8 + 1, :], (8, COLS))
            out = jnp.where((lane >> 3) == j, roll(w, 8 * j + 4), out)
            out = jnp.where((lane >> 3) == j + 6, roll(e, 8 * j + 52), out)
        return out

    def north(x, ghost):
        return jnp.where(top, ghost, roll(x, -1, 0))

    def below(x):
        return roll(x, 1, 0)

    def field(ref, f, l):
        return tile(ref, 3 * f + l)

    def fold(x, index):
        return roll(gather(x, index), 1, 0)

    def coefs(ref, ghosts, strip_ghosts):
        out = []
        ek, es, eu = (edges(tile(ref, 18 + f)) for f in (3, 4, 1))
        for l in range(LEVELS):
            u, v, k, s = (field(ref, f, l) for f in (2, 3, 4, 5))
            ke, kw = beside(k, ek, l)
            se, sw = beside(s, es, l)
            uw = beside(u, eu, l)[1]
            gs, gk = ghosts[l]
            out.append(coefficients(k, s, u, v, north(k, gk), ke, below(k), kw, north(s, gs), se, below(s), sw, uw, below(v)))
        u, v, k, s = (tile(ref, 18 + f) for f in (1, 2, 3, 4))
        gs, gk = strip_ghosts
        out.append(
            coefficients(
                k, s, u, v, north(k, gk), roll(k, -1), below(k), roll(k, 1), north(s, gs), roll(s, -1), below(s), roll(s, 1),
                roll(u, 1), below(v),
            )
        )
        return out

    def advance(c, q, strip, ghosts, strip_ghost):
        edge = edges(strip)
        out = []
        for j in range(6):
            e, w = beside(q[j], edge, j)
            out.append(stencil(c[j % 3], q[j], e, w, north(q[j], ghosts[j]), below(q[j])))
        new = stencil(c[3], strip, roll(strip, -1), roll(strip, 1), north(strip, strip_ghost), below(strip))
        return out, new

    zero = jnp.zeros((8, COLS), jnp.float32)
    d0 = [tile(d_ref, j) for j in range(6)]
    p0 = [tile(p_ref, j) for j in range(6)]
    static = [(fold(field(d_ref, 5, l), index_p), fold(field(d_ref, 4, l), index_p)) for l in range(LEVELS)]
    cp = coefs(p_ref, static, (outer(1), outer(2)))
    cd = coefs(d_ref, [(zero, zero)] * 3, (zero, zero))
    d1, _ = advance(cd, d0, tile(d_ref, 18), [zero] * 6, zero)
    p1, strip = advance(cp, p0, tile(p_ref, 18), [fold(x, index_p) for x in d0], outer(0))
    p2, strip = advance(cp, p1, strip, [fold(x, index_p) for x in d1], zero)
    p3, _ = advance(cp, p2, strip, [zero] * 6, zero)
    for j in range(6):
        l = j % 3
        values = [p0[j], p1[j], p2[j], p3[j], field(p_ref, 5, l), field(p_ref, 4, l)]
        out = zero
        for i, x in enumerate(values):
            out = jnp.where(row == i, roll(gather(x, index_d), i - 6, 0), out)
        g_ref[pl.ds(8 * j, 8), :] = out


def ghosts(partner, own, xr, yr):
    extra = pl.BlockSpec((16, COLS), lambda i: (ROWS // 16, 0))
    return pl.pallas_call(
        ghost_kernel,
        out_shape=jax.ShapeDtypeStruct((48, COLS), jnp.float32),
        grid=(1,),
        in_specs=[whole(8 * TILES + 8)] * 2 + [extra, extra],
        out_specs=whole(48),
        compiler_params=PARAMS,
        name="ghost",
    )(partner, own, xr, yr)


def steps_kernel(*refs):
    t_ref, s_ref, u_ref, v_ref, k_ref, w_ref, pt_ref, pc_ref, xr_ref, yr_ref, a_ref, b_ref, g_ref, gx_ref, gy_ref = refs[:15]
    heat_ref, salt_ref, dens_ref = refs[15:18]
    q0, q1, fields, coef = refs[18:22]
    odd = lax.rem(lax.axis_index("lon"), 2) == 1
    lat = lax.axis_index("lat")
    odd_lat = lax.rem(lat, 2) == 1
    at_top = lat == LAT - 1
    lane = iota(1)
    tracers = (t_ref, s_ref)

    def fill(i, carry):
        src = pl.ds(pl.multiple_of(i * 8, 8), 8)
        dst = pl.ds(pl.multiple_of(i * 8 + BASE, 8), 8)
        for t in range(2):
            for l in range(LEVELS):
                q0[3 * t + l, dst, :] = tracers[t][l, src, :]
        for f, ref in enumerate((u_ref, v_ref, k_ref, w_ref)):
            for l in range(LEVELS):
                x = ref[l, src, :]
                fields[4 * f + l, dst, :] = sea_of(x) if f == 3 else x
        x, y = xr_ref[src, :], yr_ref[src, :]
        mw, me = jnp.where(odd, x, y), jnp.where(odd, y, x)
        parts = strips(pt_ref[src, :], pc_ref[src, :], mw, me)
        q0[6, dst, :] = parts[0]
        for f in range(4):
            fields[4 * f + 3, dst, :] = parts[1 + f]
        return carry

    lax.fori_loop(0, ROWS // 8, fill, 0, unroll=2)

    def place(j):
        if j < 6:
            return q0, j
        if j < 18:
            return fields, 4 * ((j - 6) // 3) + j % 3
        if j == 18:
            return q0, 6
        return fields, 4 * (j - 19) + 3

    for j in range(TILES):
        a, b = a_ref[pl.ds(4 * j, 4), :], b_ref[pl.ds(4 * j, 4), :]
        ref, n = place(j)
        ref[n, pl.ds(BASE - 4, 4), :] = jnp.where(odd_lat, a, b)
        ref[n, pl.ds(NORTH, 4), :] = jnp.where(odd_lat, b, a)

    own = [g_ref[pl.ds(8 * j, 8), :] for j in range(6)]
    strip = jnp.zeros((8, COLS), jnp.float32)
    for j in range(6):
        x, y = gx_ref[pl.ds(8 * j, 8), :], gy_ref[pl.ds(8 * j, 8), :]
        west, east = jnp.where(odd, x, y), jnp.where(odd, y, x)
        strip = jnp.where((lane >> 3) == j, roll(jnp.where(lane >= COLS - 4, west, own[j]), 8 * j + 4), strip)
        strip = jnp.where((lane >> 3) == j + 6, roll(jnp.where(lane < 4, east, own[j]), 8 * j + 52), strip)

    def put(ref, s):
        @pl.when(at_top)
        def _():
            for j in range(6):
                ref[j, pl.ds(NORTH, 1), :] = own[j][s : s + 1, :]
            ref[6, pl.ds(NORTH, 1), :] = strip[s : s + 1, :]

    put(q0, 0)

    @pl.when(at_top)
    def _():
        for f, s in ((3, 4), (2, 5)):
            for l in range(LEVELS):
                fields[4 * f + l, pl.ds(NORTH, 1), :] = own[l][s : s + 1, :]
            fields[4 * f + 3, pl.ds(NORTH, 1), :] = strip[s : s + 1, :]

    def coef_block(i, carry):
        r = i * 8 + FIRST_BLOCK

        def load(f, l, shift=0):
            return fields[4 * f + l, pl.ds(r + shift, 8), :]

        ku, ks, kk = (edges(load(f, 3)) for f in (0, 3, 2))
        for l in range(4):
            u, v, k, s = (load(f, l) for f in range(4))
            if l < 3:
                ke, kw = beside(k, kk, l)
                se, sw = beside(s, ks, l)
                uw = beside(u, ku, l)[1]
            else:
                ke, kw, se, sw, uw = roll(k, -1), roll(k, 1), roll(s, -1), roll(s, 1), roll(u, 1)
            out = coefficients(
                k, s, u, v, load(2, l, 1), ke, load(2, l, -1), kw, load(3, l, 1), se, load(3, l, -1), sw, uw, load(1, l, -1)
            )
            for n in range(5):
                coef[4 * n + l, pl.ds(pl.multiple_of(r, 8), 8), :] = out[n]
        return carry

    lax.fori_loop(0, BLOCKS, coef_block, 0)

    def advance(src, r):
        rows = pl.ds(pl.multiple_of(r, 8), 8)
        strip = src[6, rows, :]
        edge = edges(strip)
        out = []
        for j in range(6):
            c = [coef[4 * n + j % 3, rows, :] for n in range(5)]
            q = src[j, rows, :]
            e, w = beside(q, edge, j)
            out.append(stencil(c, q, e, w, src[j, pl.ds(r + 1, 8), :], src[j, pl.ds(r - 1, 8), :]))
        return out, strip

    def step(src, dst):
        def block(i, carry):
            r = i * 8 + FIRST_BLOCK
            rows = pl.ds(pl.multiple_of(r, 8), 8)
            out, strip = advance(src, r)
            for j in range(6):
                dst[j, rows, :] = out[j]
            c = [coef[4 * n + 3, rows, :] for n in range(5)]
            dst[6, rows, :] = stencil(
                c, strip, roll(strip, -1), roll(strip, 1), src[6, pl.ds(r + 1, 8), :], src[6, pl.ds(r - 1, 8), :]
            )
            return carry

        lax.fori_loop(0, BLOCKS, block, 0)

    step(q0, q1)
    put(q1, 1)
    step(q1, q0)
    put(q0, 2)
    step(q0, q1)
    put(q1, 3)

    def final(i, carry):
        out, _ = advance(q1, i * 8 + BASE)
        dst = pl.ds(pl.multiple_of(i * 8, 8), 8)
        for l in range(LEVELS):
            heat, salt = out[l], out[3 + l]
            sea = sea_of(w_ref[l, dst, :])
            heat_ref[l, dst, :] = heat
            salt_ref[l, dst, :] = salt
            dens_ref[l, dst, :] = sea * (-0.2 * heat * (1.0 + 0.05 * heat) + 0.8 * salt - 0.01 * heat * salt)
        return carry

    lax.fori_loop(0, ROWS // 8, final, 0)


def four_steps(*operands):
    out = jax.ShapeDtypeStruct((LEVELS, ROWS, COLS), jnp.float32)
    return pl.pallas_call(
        steps_kernel,
        out_shape=(out, out, out),
        in_specs=vmem(len(operands)),
        out_specs=tuple(vmem(3)),
        scratch_shapes=[
            pltpu.VMEM((7, EXT, COLS), jnp.float32),
            pltpu.VMEM((7, EXT, COLS), jnp.float32),
            pltpu.VMEM((16, EXT, COLS), jnp.float32),
            pltpu.VMEM((20, EXT, COLS), jnp.float32),
        ],
        compiler_params=PARAMS,
        name="steps",
    )(*operands)


def fold_exchange(message, seam):
    rotation = (seam[0] // COLS + 1 + lax.axis_index("lon")) % LON
    far = rotation >= HALF

    def relay(x):
        return lax.cond(far, lambda y: swap(y, PAIR_A), lambda y: y, x)

    branches = [functools.partial(swap, pairs=fold_pairs(r)) for r in range(HALF)]
    return relay(lax.switch(rotation % HALF, branches, relay(message)))


def on_device(t, s, u, v, k, w, seam):
    m = seam.reshape(1, COLS)
    xs, ys, pt, pc = pack(t, s, u, v, k, w, m)
    yr = swap(ys, PAIR_Y)
    xr = swap(xs, PAIR_X)
    a, b, message = rows((t, s, u, v, k, w), pt, pc, xr, yr, m)
    partner = fold_exchange(message, seam)
    ar = swap(a, PAIR_A)
    br = swap(b, PAIR_B)
    g = ghosts(partner, message, xr, yr)
    gy = swap(g, PAIR_Y)
    gx = swap(g, PAIR_X)
    return four_steps(t, s, u, v, k, w, pt, pc, xr, yr, ar, br, g, gx, gy)


def solution(mesh):
    block = P(None, "lat", "lon")
    return jax.shard_map(
        on_device,
        mesh=mesh,
        in_specs=(block,) * 6 + (P("lon"),),
        out_specs=(block,) * 3,
        check_vma=False,
    )
```

```python
import functools

import jax
import jax.numpy as jnp
from jax import lax
from jax.experimental import pallas as pl
from jax.experimental.pallas import tpu as pltpu
from jax.sharding import PartitionSpec as P

STEPS = 4
LEVELS = 3
ROWS = 256
COLS = 128
LON = 64
LAT = 4
AXES = ("lon", "lat")
HALF = LON // 2

BASE = 16
NORTH = BASE + ROWS
EXT = 288

TILES = 23
UNROLL = 8


def flat(lon, lat):
    return (lon % LON) * LAT + lat


def lon_pairs(partner):
    return [(flat(i, a), flat(partner(i), a)) for i in range(LON) for a in range(LAT)]


PAIR_X = lon_pairs(lambda i: i ^ 1)
PAIR_Y = lon_pairs(lambda i: ((i - 1) ^ 1) + 1)
PAIR_A = [(flat(i, a), flat(i, a ^ 1)) for i in range(LON) for a in range(LAT)]
PAIR_B = [(flat(i, a), flat(i, 3 - a)) for i in range(LON) for a in (1, 2)]


def fold_pairs(r):
    top = [(flat(i, 3), flat(r - 1 - i, 3)) for i in range(LON)]
    relay = [(flat(i, 2), flat(r + HALF - 1 - i, 2)) for i in range(LON)]
    return top + relay


def swap(x, pairs):
    return lax.ppermute(x, AXES, pairs)


def iota(axis):
    return lax.broadcasted_iota(jnp.int32, (8, COLS), axis)


def roll(x, shift, axis=1):
    return pltpu.roll(x, shift % x.shape[axis], axis)


def sea_of(x):
    return x.astype(jnp.float32)


def vmem(n):
    return [pl.BlockSpec(memory_space=pltpu.VMEM)] * n


PARAMS = pltpu.CompilerParams(vmem_limit_bytes=32 << 20)


def pack_kernel(t_hbm, s_hbm, u_hbm, v_hbm, k_hbm, w_hbm, m_hbm, xs_ref, ys_ref, pt_ref, pc_ref, q_ref, f_ref, w_ref, m_ref, sems):
    odd = lax.rem(lax.axis_index("lon"), 2) == 1
    lane = iota(1)
    group = lane >> 3
    low = (lane & 7) < 4
    own = pl.ds(BASE, ROWS)

    def target(n):
        if n >= 5:
            return (w_ref, m_ref)[n - 5]
        ref = q_ref if n < 2 else f_ref
        return ref.at[pl.ds(3 * (n if n < 2 else n - 2), LEVELS), own, :]

    copies = [
        pltpu.make_async_copy(src, target(n), sems.at[n])
        for n, src in enumerate((t_hbm, s_hbm, u_hbm, v_hbm, k_hbm, w_hbm, m_hbm))
    ]
    for copy in copies:
        copy.start()

    def gathered(ref, count, rows):
        out = jnp.zeros((8, COLS), jnp.float32)
        for j in range(count):
            out = jnp.where(group == j, roll(ref[j, rows, :], 4 + 8 * j), out)
        return out

    def tracer_block(i, carry):
        rows = pl.ds(pl.multiple_of(i * 8 + BASE, 8), 8)
        pt_ref[pl.ds(pl.multiple_of(i * 8, 8), 8), :] = gathered(q_ref, 6, rows)
        return carry

    def coef_block(i, carry):
        rows = pl.ds(pl.multiple_of(i * 8, 8), 8)
        here = pl.ds(pl.multiple_of(i * 8 + BASE, 8), 8)
        for l in range(LEVELS):
            f_ref[9 + l, here, :] = sea_of(w_ref[l, rows, :])
        tracers = pt_ref[rows, :]
        coefs = gathered(f_ref, 12, here)
        pc_ref[rows, :] = coefs
        east = jnp.where(low, coefs, roll(tracers, 4))
        west = jnp.where(low, roll(tracers, -4), coefs)
        xs_ref[rows, :] = jnp.where(odd, west, east)
        ys_ref[rows, :] = jnp.where(odd, east, west)
        return carry

    copies[0].wait()
    copies[1].wait()
    lax.fori_loop(0, ROWS // 8, tracer_block, 0, unroll=8)
    for copy in copies[2:]:
        copy.wait()
    lax.fori_loop(0, ROWS // 8, coef_block, 0, unroll=4)
    second = pl.ds(BASE + ROWS - 2, 1)
    for out in (xs_ref, ys_ref):
        for n in range(6):
            out[pl.ds(ROWS + n, 1), :] = q_ref[n, second, :]
        for l in range(LEVELS):
            out[pl.ds(ROWS + 6 + l, 1), :] = f_ref[9 + l, second, :]
            out[pl.ds(ROWS + 9 + l, 1), :] = f_ref[6 + l, second, :]
        out[pl.ds(ROWS + 12, 1), :] = m_ref[...].astype(jnp.float32)
        out[pl.ds(ROWS + 13, 3), :] = jnp.zeros((3, COLS), jnp.float32)


def pack(t, s, u, v, k, w, m):
    edge = jax.ShapeDtypeStruct((ROWS + 16, COLS), jnp.float32)
    own = jax.ShapeDtypeStruct((ROWS, COLS), jnp.float32)
    return pl.pallas_call(
        pack_kernel,
        out_shape=(
            edge,
            edge,
            own,
            own,
            jax.ShapeDtypeStruct((6, EXT, COLS), jnp.float32),
            jax.ShapeDtypeStruct((12, EXT, COLS), jnp.float32),
        ),
        in_specs=[pl.BlockSpec(memory_space=pltpu.HBM)] * 7,
        out_specs=tuple(vmem(6)),
        scratch_shapes=[
            pltpu.VMEM((LEVELS, ROWS, COLS), jnp.int32),
            pltpu.VMEM((1, COLS), jnp.int32),
            pltpu.SemaphoreType.DMA((7,)),
        ],
        compiler_params=PARAMS,
        name="pack",
    )(*(pltpu.with_memory_space_constraint(x, pltpu.HBM) for x in (t, s, u, v, k, w, m)))


def strips(pt, pc, mw, me):
    lane = iota(1)
    low = (lane & 7) < 4
    wt = jnp.where(low, roll(mw, -4), pt)
    et = jnp.where(low, pt, roll(me, 4))
    wc = jnp.where(low, mw, pc)
    ec = jnp.where(low, pc, me)
    out = [jnp.where(lane < 48, wt, roll(et, 48))]
    for f in range(4):
        west = jnp.where(lane < 24, roll(wc, -24 * f), roll(wc, 24 - 24 * f))
        east = jnp.where(lane < 72, roll(ec, 48 - 24 * f), roll(ec, 72 - 24 * f))
        out.append(jnp.where(lane < 48, west, east))
    return out


def rows_kernel(q_ref, fields, pt_ref, pc_ref, xs_ref, xr_ref, yr_ref, a_ref, b_ref, f_ref):
    odd = lax.rem(lax.axis_index("lon"), 2) == 1
    odd_lat = lax.rem(lax.axis_index("lat"), 2) == 1

    def tiles(start):
        rows = pl.ds(start, 8)
        here = pl.ds(start + BASE, 8)
        x, y = xr_ref[rows, :], yr_ref[rows, :]
        mw, me = jnp.where(odd, x, y), jnp.where(odd, y, x)
        main = [q_ref[n, here, :] for n in range(6)] + [fields[n, here, :] for n in range(12)]
        return main + strips(pt_ref[rows, :], pc_ref[rows, :], mw, me)

    top = tiles(ROWS - 8)
    bottom = tiles(0)
    for j in range(TILES):
        f_ref[pl.ds(8 * j, 8), :] = top[j]
        up, down = top[j][4:8, :], bottom[j][0:4, :]
        a_ref[pl.ds(4 * j, 4), :] = jnp.where(odd_lat, down, up)
        b_ref[pl.ds(4 * j, 4), :] = jnp.where(odd_lat, up, down)
    a_ref[pl.ds(4 * TILES, 4), :] = jnp.zeros((4, COLS), jnp.float32)
    b_ref[pl.ds(4 * TILES, 4), :] = jnp.zeros((4, COLS), jnp.float32)
    x, y = xr_ref[pl.ds(ROWS + 8, 8), :], yr_ref[pl.ds(ROWS + 8, 8), :]
    ew, ee = jnp.where(odd, x, y), jnp.where(odd, y, x)
    row = iota(0)
    own = jnp.broadcast_to(xs_ref[pl.ds(ROWS + 12, 1), :], (8, COLS))
    west = jnp.broadcast_to(ew[4:5, :], (8, COLS))
    east = jnp.broadcast_to(ee[4:5, :], (8, COLS))
    f_ref[pl.ds(8 * TILES, 8), :] = jnp.where(row == 0, own, jnp.where(row == 1, west, east))


def rows(q, fields, pt, pc, xs, xr, yr):
    msg = jax.ShapeDtypeStruct((4 * TILES + 4, COLS), jnp.float32)
    return pl.pallas_call(
        rows_kernel,
        out_shape=(msg, msg, jax.ShapeDtypeStruct((8 * TILES + 8, COLS), jnp.float32)),
        in_specs=vmem(7),
        out_specs=tuple(vmem(3)),
        compiler_params=PARAMS,
        name="rows",
    )(q, fields, pt, pc, xs, xr, yr)


def coefficients(k, s, u, v, kn, ke, ks, kw, sn, se, ss, sw, uw, vs):
    zero = jnp.zeros_like(k)
    fe, fw, fn, fs = 0.5 * (k + ke), 0.5 * (kw + k), 0.5 * (k + kn), 0.5 * (ks + k)
    oe, ow, on, os = s * se, sw * s, s * sn, ss * s
    ae, be = oe * (jnp.maximum(u, zero) + fe), oe * (jnp.minimum(u, zero) - fe)
    aw, bw = ow * (jnp.maximum(uw, zero) + fw), ow * (jnp.minimum(uw, zero) - fw)
    an, bn = on * (jnp.maximum(v, zero) + fn), on * (jnp.minimum(v, zero) - fn)
    a_s, bs = os * (jnp.maximum(vs, zero) + fs), os * (jnp.minimum(vs, zero) - fs)
    centre = s - (ae - bw) - (an - bs)
    return centre, -be, aw, -bn, a_s


def stencil(c, q, e, w, n, s):
    return c[0] * q + c[1] * e + c[2] * w + c[3] * n + c[4] * s


def edges(strip):
    return jnp.where((iota(1) & 7) == 3, strip, roll(strip, -50))


def beside(x, edge, j):
    lane = iota(1)
    z = roll(edge, -(8 * j + 3))
    return jnp.where(lane == COLS - 1, z, roll(x, -1)), jnp.where(lane == 0, z, roll(x, 1))


def gather(x, index):
    return jnp.take_along_axis(x, index, axis=1)


def ghost_kernel(p_ref, d_ref, xe_ref, ye_ref, g_ref):
    odd = lax.rem(lax.axis_index("lon"), 2) == 1
    row, lane = iota(0), iota(1)
    top = row == 7

    def tile(ref, j):
        return ref[pl.ds(8 * j, 8), :]

    def spread(index_row):
        return jnp.broadcast_to(index_row.astype(jnp.int32) & (COLS - 1), (8, COLS))

    index_d = spread(d_ref[pl.ds(8 * TILES, 1), :])
    index_p = spread(p_ref[pl.ds(8 * TILES, 1), :])
    index_pw = spread(p_ref[pl.ds(8 * TILES + 1, 1), :])
    index_pe = spread(p_ref[pl.ds(8 * TILES + 2, 1), :])
    xe0, ye0 = xe_ref[pl.ds(ROWS, 8), :], ye_ref[pl.ds(ROWS, 8), :]
    xe1, ye1 = xe_ref[pl.ds(ROWS + 8, 8), :], ye_ref[pl.ds(ROWS + 8, 8), :]
    east = [gather(jnp.where(odd, y, x), index_pw) for x, y in ((xe0, ye0), (xe1, ye1))]
    west = [gather(jnp.where(odd, x, y), index_pe) for x, y in ((xe0, ye0), (xe1, ye1))]

    def outer(kind):
        out = jnp.zeros((8, COLS), jnp.float32)
        for j in range(6):
            n = (j, 6 + j % 3, 9 + j % 3)[kind]
            w = jnp.broadcast_to(east[n // 8][n % 8 : n % 8 + 1, :], (8, COLS))
            e = jnp.broadcast_to(west[n // 8][n % 8 : n % 8 + 1, :], (8, COLS))
            out = jnp.where((lane >> 3) == j, roll(w, 8 * j + 4), out)
            out = jnp.where((lane >> 3) == j + 6, roll(e, 8 * j + 52), out)
        return out

    def north(x, ghost):
        return jnp.where(top, ghost, roll(x, -1, 0))

    def below(x):
        return roll(x, 1, 0)

    def field(ref, f, l):
        return tile(ref, 3 * f + l)

    def fold(x, index):
        return roll(gather(x, index), 1, 0)

    def coefs(ref, ghosts, strip_ghosts):
        out = []
        ek, es, eu = (edges(tile(ref, 18 + f)) for f in (3, 4, 1))
        for l in range(LEVELS):
            u, v, k, s = (field(ref, f, l) for f in (2, 3, 4, 5))
            ke, kw = beside(k, ek, l)
            se, sw = beside(s, es, l)
            uw = beside(u, eu, l)[1]
            gs, gk = ghosts[l]
            out.append(coefficients(k, s, u, v, north(k, gk), ke, below(k), kw, north(s, gs), se, below(s), sw, uw, below(v)))
        u, v, k, s = (tile(ref, 18 + f) for f in (1, 2, 3, 4))
        gs, gk = strip_ghosts
        out.append(
            coefficients(
                k, s, u, v, north(k, gk), roll(k, -1), below(k), roll(k, 1), north(s, gs), roll(s, -1), below(s), roll(s, 1),
                roll(u, 1), below(v),
            )
        )
        return out

    def advance(c, q, strip, ghosts, strip_ghost):
        edge = edges(strip)
        out = []
        for j in range(6):
            e, w = beside(q[j], edge, j)
            out.append(stencil(c[j % 3], q[j], e, w, north(q[j], ghosts[j]), below(q[j])))
        new = stencil(c[3], strip, roll(strip, -1), roll(strip, 1), north(strip, strip_ghost), below(strip))
        return out, new

    zero = jnp.zeros((8, COLS), jnp.float32)
    d0 = [tile(d_ref, j) for j in range(6)]
    p0 = [tile(p_ref, j) for j in range(6)]
    static = [(fold(field(d_ref, 5, l), index_p), fold(field(d_ref, 4, l), index_p)) for l in range(LEVELS)]
    cp = coefs(p_ref, static, (outer(1), outer(2)))
    cd = coefs(d_ref, [(zero, zero)] * 3, (zero, zero))
    d1, _ = advance(cd, d0, tile(d_ref, 18), [zero] * 6, zero)
    p1, strip = advance(cp, p0, tile(p_ref, 18), [fold(x, index_p) for x in d0], outer(0))
    p2, strip = advance(cp, p1, strip, [fold(x, index_p) for x in d1], zero)
    p3, _ = advance(cp, p2, strip, [zero] * 6, zero)
    for j in range(6):
        l = j % 3
        values = [p0[j], p1[j], p2[j], p3[j], field(p_ref, 5, l), field(p_ref, 4, l)]
        out = zero
        for i, x in enumerate(values):
            out = jnp.where(row == i, roll(gather(x, index_d), i - 6, 0), out)
        g_ref[pl.ds(8 * j, 8), :] = out


def ghosts(partner, own, xr, yr):
    return pl.pallas_call(
        ghost_kernel,
        out_shape=jax.ShapeDtypeStruct((48, COLS), jnp.float32),
        in_specs=vmem(4),
        out_specs=vmem(1)[0],
        compiler_params=PARAMS,
        name="ghost",
    )(partner, own, xr, yr)


def coef_block(load, store):
    ku, ks, kk = (load(f, 4, 0) for f in (0, 3, 2))
    for l in range(4):
        u, v, k, s = (load(f, l, 0) for f in range(4))
        if l < 3:
            ke, kw = beside(k, kk, l)
            se, sw = beside(s, ks, l)
            uw = beside(u, ku, l)[1]
        else:
            ke, kw, se, sw, uw = roll(k, -1), roll(k, 1), roll(s, -1), roll(s, 1), roll(u, 1)
        out = coefficients(
            k, s, u, v, load(2, l, 1), ke, load(2, l, -1), kw, load(3, l, 1), se, load(3, l, -1), sw, uw, load(1, l, -1)
        )
        for n in range(5):
            store(n, l, out[n])


def advance(load, c, last):
    edge = load(7, 0)
    out = []
    for j in range(6):
        q = load(j, 0)
        e, w = beside(q, edge, j)
        out.append(stencil([c(n, j % 3) for n in range(5)], q, e, w, load(j, 1), load(j, -1)))
    if not last:
        strip = load(6, 0)
        strip_c = [c(n, 3) for n in range(5)]
        new = stencil(strip_c, strip, roll(strip, -1), roll(strip, 1), load(6, 1), load(6, -1))
        out += [new, edges(new)]
    return out


def outputs(out, sea, store):
    for l in range(LEVELS):
        heat, salt = out[l], out[3 + l]
        dens = sea(l) * (-0.2 * heat * (1.0 + 0.05 * heat) + 0.8 * salt - 0.01 * heat * salt)
        for n, x in enumerate((heat, salt, dens)):
            store(n, l, x)


def eight(r):
    return pl.ds(pl.multiple_of(r, 8), 8)


def main_kernel(q_ref, fields, pt_ref, pc_ref, xr_ref, yr_ref, heat_ref, salt_ref, dens_ref, strip_ref, edge_ref, coef, qa, qb):
    odd = lax.rem(lax.axis_index("lon"), 2) == 1
    results = (heat_ref, salt_ref, dens_ref)

    def fill(i, carry):
        src = eight(i * 8)
        x, y = xr_ref[src, :], yr_ref[src, :]
        mw, me = jnp.where(odd, x, y), jnp.where(odd, y, x)
        for n, part in enumerate(strips(pt_ref[src, :], pc_ref[src, :], mw, me)):
            strip_ref[n, eight(i * 8 + BASE), :] = part
            if n != 2:
                edge_ref[n, eight(i * 8 + BASE), :] = edges(part)
        return carry

    lax.fori_loop(0, ROWS // 8, fill, 0, unroll=UNROLL)

    def block(i, carry):
        r = i * 8 + BASE

        def load(f, l, shift):
            rows = pl.ds(r + shift, 8)
            if l == 4:
                return edge_ref[1 + f, rows, :]
            return strip_ref[1 + f, rows, :] if l == 3 else fields[3 * f + l, rows, :]

        def store(n, l, x):
            coef[4 * n + l, eight(r), :] = x

        coef_block(load, store)
        return carry

    lax.fori_loop(0, ROWS // 8, block, 0, unroll=4)

    def loader(src, r):
        def load(j, shift):
            rows = pl.ds(r + shift, 8)
            if src is not None:
                return src[j, rows, :]
            return q_ref[j, rows, :] if j < 6 else (strip_ref, edge_ref)[j - 6][0, rows, :]

        return load

    def coefficient(r):
        return lambda n, l: coef[4 * n + l, eight(r), :]

    for src, dst in ((None, qa), (qa, qb), (qb, qa)):

        def block(i, carry):
            r = i * 8 + BASE
            for j, x in enumerate(advance(loader(src, r), coefficient(r), False)):
                dst[j, eight(r), :] = x
            return carry

        lax.fori_loop(0, ROWS // 8, block, 0, unroll=UNROLL)

    def final(i, carry):
        r = i * 8 + BASE
        rows = eight(i * 8)

        def store(n, l, x):
            results[n][l, rows, :] = x

        outputs(advance(loader(qa, r), coefficient(r), True), lambda l: fields[9 + l, eight(r), :], store)
        return carry

    lax.fori_loop(0, ROWS // 8, final, 0, unroll=UNROLL)


def inner_steps(q, fields, pt, pc, xr, yr):
    out = jax.ShapeDtypeStruct((LEVELS, ROWS, COLS), jnp.float32)
    return pl.pallas_call(
        main_kernel,
        out_shape=(out, out, out, jax.ShapeDtypeStruct((5, EXT, COLS), jnp.float32)),
        in_specs=vmem(6),
        out_specs=tuple(vmem(4)),
        scratch_shapes=[
            pltpu.VMEM((5, EXT, COLS), jnp.float32),
            pltpu.VMEM((20, EXT, COLS), jnp.float32),
            pltpu.VMEM((8, EXT, COLS), jnp.float32),
            pltpu.VMEM((8, EXT, COLS), jnp.float32),
        ],
        compiler_params=PARAMS,
        cost_estimate=pl.CostEstimate(flops=60_000_000, bytes_accessed=36_000_000, transcendentals=0),
        name="main",
    )(q, fields, pt, pc, xr, yr)


ZONE = 64
SHIFT = NORTH - 48
SOUTH_BLOCKS = (8, 16, 24)
NORTH_BLOCKS = (32, 40, 48)


def zone_kernel(q_ref, fields, strip_ref, a_ref, b_ref, g_ref, gx_ref, gy_ref, h_in, s_in, d_in, h_out, s_out, d_out, *scratch):
    zq, zr, zf, zc, patch, sems = scratch
    odd = lax.rem(lax.axis_index("lon"), 2) == 1
    lat = lax.axis_index("lat")
    odd_lat = lax.rem(lat, 2) == 1
    at_top = lat == LAT - 1
    lane = iota(1)

    def place(j):
        if j < 6:
            return zq, j, q_ref, j
        if j < 18:
            return zf, 4 * ((j - 6) // 3) + j % 3, fields, j - 6
        if j == 18:
            return zq, 6, strip_ref, 0
        return zf, 4 * (j - 19) + 3, strip_ref, j - 18

    for j in range(TILES):
        ref, n, src, m = place(j)
        ref[n, pl.ds(BASE, 16), :] = src[m, pl.ds(BASE, 16), :]
        ref[n, pl.ds(32, 16), :] = src[m, pl.ds(NORTH - 16, 16), :]
        a, b = a_ref[pl.ds(4 * j, 4), :], b_ref[pl.ds(4 * j, 4), :]
        ref[n, pl.ds(BASE - 4, 4), :] = jnp.where(odd_lat, a, b)
        ref[n, pl.ds(48, 4), :] = jnp.where(odd_lat, b, a)

    own = [g_ref[pl.ds(8 * j, 8), :] for j in range(6)]
    strip = jnp.zeros((8, COLS), jnp.float32)
    for j in range(6):
        x, y = gx_ref[pl.ds(8 * j, 8), :], gy_ref[pl.ds(8 * j, 8), :]
        west, east = jnp.where(odd, x, y), jnp.where(odd, y, x)
        strip = jnp.where((lane >> 3) == j, roll(jnp.where(lane >= COLS - 4, west, own[j]), 8 * j + 4), strip)
        strip = jnp.where((lane >> 3) == j + 6, roll(jnp.where(lane < 4, east, own[j]), 8 * j + 52), strip)

    ghost = pl.ds(48, 1)

    def put(ref, s):
        @pl.when(at_top)
        def _():
            for j in range(6):
                ref[j, ghost, :] = own[j][s : s + 1, :]
            ref[6, ghost, :] = strip[s : s + 1, :]

    put(zq, 0)

    @pl.when(at_top)
    def _():
        for f, s in ((3, 4), (2, 5)):
            for l in range(LEVELS):
                zf[4 * f + l, ghost, :] = own[l][s : s + 1, :]
            zf[4 * f + 3, ghost, :] = strip[s : s + 1, :]

    for r in SOUTH_BLOCKS + NORTH_BLOCKS:

        def load(f, l, shift):
            return zf[4 * f + l, pl.ds(r + shift, 8), :]

        def store(n, l, x):
            zc[4 * n + l, pl.ds(r, 8), :] = x

        def with_edges(f, l, shift):
            return edges(load(f, 3, shift)) if l == 4 else load(f, l, shift)

        coef_block(with_edges, store)

    def loader(src, r):
        def load(j, shift):
            return edges(src[6, pl.ds(r, 8), :]) if j == 7 else src[j, pl.ds(r + shift, 8), :]

        return load

    def coefficient(r):
        return lambda n, l: zc[4 * n + l, pl.ds(r, 8), :]

    for s, (src, dst) in enumerate(((zq, zr), (zr, zq), (zq, zr))):
        for r in SOUTH_BLOCKS + NORTH_BLOCKS:
            out = advance(loader(src, r), coefficient(r), False)
            for j, x in enumerate(out[:7]):
                dst[j, pl.ds(r, 8), :] = x
        put(dst, s + 1)

    copies = []
    for z, (r, row) in enumerate(((16, 0), (40, ROWS - 8))):

        def store(n, l, x):
            patch[2 * n + z, l, :, :] = x

        out = advance(loader(zr, r), coefficient(r), True)
        outputs(out, lambda l: zf[12 + l, pl.ds(r, 8), :], store)
        for n, ref in enumerate((h_out, s_out, d_out)):
            copy = pltpu.make_async_copy(patch.at[2 * n + z], ref.at[:, pl.ds(row, 8), :], sems.at[2 * n + z])
            copy.start()
            copies.append(copy)
    for copy in copies:
        copy.wait()


def zones(q, fields, strip, a, b, g, gx, gy, *results):
    out = jax.ShapeDtypeStruct((LEVELS, ROWS, COLS), jnp.float32)
    anywhere = [pl.BlockSpec(memory_space=pl.ANY)] * 3
    return pl.pallas_call(
        zone_kernel,
        out_shape=(out, out, out),
        in_specs=vmem(8) + anywhere,
        out_specs=tuple(anywhere),
        scratch_shapes=[
            pltpu.VMEM((7, ZONE, COLS), jnp.float32),
            pltpu.VMEM((7, ZONE, COLS), jnp.float32),
            pltpu.VMEM((16, ZONE, COLS), jnp.float32),
            pltpu.VMEM((20, ZONE, COLS), jnp.float32),
            pltpu.VMEM((6, LEVELS, 8, COLS), jnp.float32),
            pltpu.SemaphoreType.DMA((6,)),
        ],
        input_output_aliases={8: 0, 9: 1, 10: 2},
        compiler_params=PARAMS,
        name="zones",
    )(q, fields, strip, a, b, g, gx, gy, *results)


def fold_exchange(message, seam):
    rotation = (seam[0] // COLS + 1 + lax.axis_index("lon")) % LON
    far = rotation >= HALF

    def relay(x):
        return lax.cond(far, lambda y: swap(y, PAIR_A), lambda y: y, x)

    branches = [functools.partial(swap, pairs=fold_pairs(r)) for r in range(HALF)]
    return relay(lax.switch(rotation % HALF, branches, relay(message)))


def on_device(t, s, u, v, k, w, seam):
    m = seam.reshape(1, COLS)
    xs, ys, pt, pc, q, fields = pack(t, s, u, v, k, w, m)
    yr = swap(ys, PAIR_Y)
    xr = swap(xs, PAIR_X)
    a, b, message = rows(q, fields, pt, pc, xs, xr, yr)
    partner = fold_exchange(message, seam)
    g = ghosts(partner, message, xr, yr)
    gy = swap(g, PAIR_Y)
    gx = swap(g, PAIR_X)
    a, b, _ = lax.optimization_barrier((a, b, g))
    br = swap(b, PAIR_B)
    ar = swap(a, PAIR_A)
    *results, strip = inner_steps(q, fields, pt, pc, xr, yr)
    return zones(q, fields, strip, ar, br, g, gx, gy, *results)


def solution(mesh):
    block = P(None, "lat", "lon")
    return jax.shard_map(
        on_device,
        mesh=mesh,
        in_specs=(block,) * 6 + (P("lon"),),
        out_specs=(block,) * 3,
        check_vma=False,
    )
```

```python
import functools

import jax
import jax.numpy as jnp
from jax import lax
from jax.experimental import pallas as pl
from jax.experimental.pallas import tpu as pltpu
from jax.sharding import PartitionSpec as P

STEPS = 4
LEVELS = 3
ROWS = 256
COLS = 128
LON = 64
LAT = 4
AXES = ("lon", "lat")
HOP = 8

BASE = 16
NORTH = BASE + ROWS
EXT = 288

TILES = 23
UNROLL = 8

SEAM = 5 * TILES + 3
FOLD_ROWS = 128
PACKED = 18
ROW_ROWS = 4 * 20
GHOST_ROWS = 48


def flat(lon, lat):
    return (lon % LON) * LAT + lat


def lon_pairs(partner):
    return [(flat(i, a), flat(partner(i), a)) for i in range(LON) for a in range(LAT)]


PAIR_X = lon_pairs(lambda i: i ^ 1)
PAIR_Y = lon_pairs(lambda i: ((i - 1) ^ 1) + 1)
PAIR_A = [(flat(i, a), flat(i, a ^ 1)) for i in range(LON) for a in range(LAT)]
PAIR_B = [(flat(i, a), flat(i, 3 - a)) for i in range(LON) for a in (1, 2)]


PAIR_HOP = [(flat(i, LAT - 1), flat(i + HOP, LAT - 1)) for i in range(LON)]


def fold_pairs(r):
    return [(flat(i, LAT - 1), flat(r - 1 - i, LAT - 1)) for i in range(LON)]


def swap(x, pairs):
    return lax.ppermute(x, AXES, pairs)


def iota(axis):
    return lax.broadcasted_iota(jnp.int32, (8, COLS), axis)


def roll(x, shift, axis=1):
    return pltpu.roll(x, shift % x.shape[axis], axis)


def sea_of(x):
    return x.astype(jnp.float32)


def vmem(n):
    return [pl.BlockSpec(memory_space=pltpu.VMEM)] * n


PARAMS = pltpu.CompilerParams(vmem_limit_bytes=32 << 20)


def pack_kernel(t_hbm, s_hbm, u_hbm, v_hbm, k_hbm, w_hbm, m_hbm, xs_ref, ys_ref, pt_ref, pc_ref, q_ref, f_ref, w_ref, m_ref, sems):
    odd = lax.rem(lax.axis_index("lon"), 2) == 1
    group = iota(1) >> 3
    own = pl.ds(BASE, ROWS)

    def target(n):
        if n >= 5:
            return (w_ref, m_ref)[n - 5]
        ref = q_ref if n < 2 else f_ref
        return ref.at[pl.ds(3 * (n if n < 2 else n - 2), LEVELS), own, :]

    copies = [
        pltpu.make_async_copy(src, target(n), sems.at[n])
        for n, src in enumerate((t_hbm, s_hbm, u_hbm, v_hbm, k_hbm, w_hbm, m_hbm))
    ]
    for copy in copies:
        copy.start()

    def gathered(ref, count, rows):
        out = jnp.zeros((8, COLS), jnp.float32)
        for j in range(count):
            out = jnp.where(group == j, roll(ref[j, rows, :], 4 + 8 * j), out)
        return out

    def tracer_block(i, carry):
        rows = pl.ds(pl.multiple_of(i * 8 + BASE, 8), 8)
        pt_ref[pl.ds(pl.multiple_of(i * 8, 8), 8), :] = gathered(q_ref, 6, rows)
        return carry

    def coef_block(i, carry):
        rows = pl.ds(pl.multiple_of(i * 8, 8), 8)
        here = pl.ds(pl.multiple_of(i * 8 + BASE, 8), 8)
        for l in range(LEVELS):
            f_ref[9 + l, here, :] = sea_of(w_ref[l, rows, :])
        tracers = pt_ref[rows, :]
        coefs = gathered(f_ref, 12, here)
        pc_ref[rows, :] = coefs
        east, west = edge_message(tracers, coefs)
        xs_ref[rows, :] = jnp.where(odd, west, east)
        ys_ref[rows, :] = jnp.where(odd, east, west)
        return carry

    copies[0].wait()
    copies[1].wait()
    lax.fori_loop(0, ROWS // 8, tracer_block, 0, unroll=8)
    for copy in copies[2:]:
        copy.wait()
    lax.fori_loop(0, ROWS // 8, coef_block, 0, unroll=4)
    second = pl.ds(BASE + ROWS - 2, 1)
    for out in (xs_ref, ys_ref):
        for n in range(6):
            out[pl.ds(ROWS + n, 1), :] = q_ref[n, second, :]
        for l in range(LEVELS):
            out[pl.ds(ROWS + 6 + l, 1), :] = f_ref[9 + l, second, :]
            out[pl.ds(ROWS + 9 + l, 1), :] = f_ref[6 + l, second, :]
        out[pl.ds(ROWS + 12, 1), :] = m_ref[...].astype(jnp.float32)
        out[pl.ds(ROWS + 13, 3), :] = jnp.zeros((3, COLS), jnp.float32)


def pack(t, s, u, v, k, w, m):
    edge = jax.ShapeDtypeStruct((ROWS + 16, COLS), jnp.float32)
    own = jax.ShapeDtypeStruct((ROWS, COLS), jnp.float32)
    return pl.pallas_call(
        pack_kernel,
        out_shape=(
            edge,
            edge,
            own,
            own,
            jax.ShapeDtypeStruct((6, EXT, COLS), jnp.float32),
            jax.ShapeDtypeStruct((12, EXT, COLS), jnp.float32),
        ),
        in_specs=[pl.BlockSpec(memory_space=pltpu.HBM)] * 7,
        out_specs=tuple(vmem(6)),
        scratch_shapes=[
            pltpu.VMEM((LEVELS, ROWS, COLS), jnp.int32),
            pltpu.VMEM((1, COLS), jnp.int32),
            pltpu.SemaphoreType.DMA((7,)),
        ],
        compiler_params=PARAMS,
        name="pack",
    )(*(pltpu.with_memory_space_constraint(x, pltpu.HBM) for x in (t, s, u, v, k, w, m)))


def rows_kernel(q_ref, fields, pt_ref, pc_ref, a_ref, b_ref):
    odd_lat = lax.rem(lax.axis_index("lat"), 2) == 1
    for j in range(20):
        if j < 18:
            ref, n = (q_ref, j) if j < 6 else (fields, j - 6)
            down, up = ref[n, pl.ds(BASE, 8), :][0:4], ref[n, pl.ds(NORTH - 8, 8), :][4:8]
        else:
            ref = (pt_ref, pc_ref)[j - 18]
            down, up = ref[pl.ds(0, 8), :][0:4], ref[pl.ds(ROWS - 8, 8), :][4:8]
        a_ref[pl.ds(4 * j, 4), :] = jnp.where(odd_lat, down, up)
        b_ref[pl.ds(4 * j, 4), :] = jnp.where(odd_lat, up, down)


def edge_rows(q, fields, pt, pc):
    return pl.pallas_call(
        rows_kernel,
        out_shape=(jax.ShapeDtypeStruct((ROW_ROWS, COLS), jnp.float32),) * 2,
        in_specs=vmem(4),
        out_specs=tuple(vmem(2)),
        compiler_params=PARAMS,
        name="rows",
    )(q, fields, pt, pc)


def edge_message(tracers, coefs):
    low = (iota(1) & 7) < 4
    return jnp.where(low, coefs, roll(tracers, 4)), jnp.where(low, roll(tracers, -4), coefs)


def halo_tile(a_ref, b_ref, j):
    odd_lat = lax.rem(lax.axis_index("lat"), 2) == 1
    a, b = a_ref[pl.ds(4 * j, 4), :], b_ref[pl.ds(4 * j, 4), :]
    return jnp.concatenate([jnp.where(odd_lat, a, b), jnp.where(odd_lat, b, a)], axis=0)


def strips(pt, pc, mw, me):
    lane = iota(1)
    low = (lane & 7) < 4
    wt = jnp.where(low, roll(mw, -4), pt)
    et = jnp.where(low, pt, roll(me, 4))
    wc = jnp.where(low, mw, pc)
    ec = jnp.where(low, pc, me)
    out = [jnp.where(lane < 48, wt, roll(et, 48))]
    for f in range(4):
        west = jnp.where(lane < 24, roll(wc, -24 * f), roll(wc, 24 - 24 * f))
        east = jnp.where(lane < 72, roll(ec, 48 - 24 * f), roll(ec, 72 - 24 * f))
        out.append(jnp.where(lane < 48, west, east))
    return out


def top_kernel(q_ref, fields, pt_ref, pc_ref, xs_ref, xr_ref, yr_ref, f_ref):
    odd = lax.rem(lax.axis_index("lon"), 2) == 1
    rows = pl.ds(ROWS - 8, 8)
    here = pl.ds(NORTH - 8, 8)
    x, y = xr_ref[rows, :], yr_ref[rows, :]
    mw, me = jnp.where(odd, x, y), jnp.where(odd, y, x)
    tiles = [q_ref[n, here, :] for n in range(6)] + [fields[n, here, :] for n in range(12)]
    tiles += strips(pt_ref[rows, :], pc_ref[rows, :], mw, me)
    f_ref[pl.ds(0, 3), :] = jnp.zeros((3, COLS), jnp.float32)
    for j in range(TILES):
        f_ref[pl.ds(5 * j + 3, 5), :] = tiles[j][3:8, :]
    x, y = xr_ref[pl.ds(ROWS + 8, 8), :], yr_ref[pl.ds(ROWS + 8, 8), :]
    ew, ee = jnp.where(odd, x, y), jnp.where(odd, y, x)
    f_ref[pl.ds(SEAM, 1), :] = xs_ref[pl.ds(ROWS + 12, 1), :]
    f_ref[pl.ds(SEAM + 1, 1), :] = ew[4:5, :]
    f_ref[pl.ds(SEAM + 2, 1), :] = ee[4:5, :]
    f_ref[pl.ds(SEAM + 3, FOLD_ROWS - SEAM - 3), :] = jnp.zeros((FOLD_ROWS - SEAM - 3, COLS), jnp.float32)


def top_rows(q, fields, pt, pc, xs, xr, yr):
    return pl.pallas_call(
        top_kernel,
        out_shape=jax.ShapeDtypeStruct((FOLD_ROWS, COLS), jnp.float32),
        in_specs=vmem(7),
        out_specs=vmem(1)[0],
        compiler_params=PARAMS,
        name="top",
    )(q, fields, pt, pc, xs, xr, yr)


def coefficients(k, s, u, v, kn, ke, ks, kw, sn, se, ss, sw, uw, vs):
    zero = jnp.zeros_like(k)
    fe, fw, fn, fs = 0.5 * (k + ke), 0.5 * (kw + k), 0.5 * (k + kn), 0.5 * (ks + k)
    oe, ow, on, os = s * se, sw * s, s * sn, ss * s
    ae, be = oe * (jnp.maximum(u, zero) + fe), oe * (jnp.minimum(u, zero) - fe)
    aw, bw = ow * (jnp.maximum(uw, zero) + fw), ow * (jnp.minimum(uw, zero) - fw)
    an, bn = on * (jnp.maximum(v, zero) + fn), on * (jnp.minimum(v, zero) - fn)
    a_s, bs = os * (jnp.maximum(vs, zero) + fs), os * (jnp.minimum(vs, zero) - fs)
    centre = s - (ae - bw) - (an - bs)
    return centre, -be, aw, -bn, a_s


def stencil(c, q, e, w, n, s):
    return c[0] * q + c[1] * e + c[2] * w + c[3] * n + c[4] * s


def edges(strip):
    return jnp.where((iota(1) & 7) == 3, strip, roll(strip, -50))


def beside(x, edge, j):
    lane = iota(1)
    z = roll(edge, -(8 * j + 3))
    return jnp.where(lane == COLS - 1, z, roll(x, -1)), jnp.where(lane == 0, z, roll(x, 1))


def gather(x, index):
    return jnp.take_along_axis(x, index, axis=1)


def ghost_kernel(p_ref, d_ref, xe_ref, ye_ref, a_ref, b_ref, gx_ref, gy_ref):
    odd = lax.rem(lax.axis_index("lon"), 2) == 1
    row, lane = iota(0), iota(1)
    top = row == 7

    def tile(ref, j):
        return ref[pl.ds(5 * j, 8), :]

    def spread(index_row):
        return jnp.broadcast_to(index_row.astype(jnp.int32) & (COLS - 1), (8, COLS))

    index_d = spread(d_ref[pl.ds(SEAM, 1), :])
    index_p = spread(p_ref[pl.ds(SEAM, 1), :])
    index_pw = spread(p_ref[pl.ds(SEAM + 1, 1), :])
    index_pe = spread(p_ref[pl.ds(SEAM + 2, 1), :])
    xe0, ye0 = xe_ref[pl.ds(ROWS, 8), :], ye_ref[pl.ds(ROWS, 8), :]
    xe1, ye1 = xe_ref[pl.ds(ROWS + 8, 8), :], ye_ref[pl.ds(ROWS + 8, 8), :]
    east = [gather(jnp.where(odd, y, x), index_pw) for x, y in ((xe0, ye0), (xe1, ye1))]
    west = [gather(jnp.where(odd, x, y), index_pe) for x, y in ((xe0, ye0), (xe1, ye1))]

    def outer(kind):
        out = jnp.zeros((8, COLS), jnp.float32)
        for j in range(6):
            n = (j, 6 + j % 3, 9 + j % 3)[kind]
            w = jnp.broadcast_to(east[n // 8][n % 8 : n % 8 + 1, :], (8, COLS))
            e = jnp.broadcast_to(west[n // 8][n % 8 : n % 8 + 1, :], (8, COLS))
            out = jnp.where((lane >> 3) == j, roll(w, 8 * j + 4), out)
            out = jnp.where((lane >> 3) == j + 6, roll(e, 8 * j + 52), out)
        return out

    def north(x, ghost):
        return jnp.where(top, ghost, roll(x, -1, 0))

    def below(x):
        return roll(x, 1, 0)

    def field(ref, f, l):
        return tile(ref, 3 * f + l)

    def fold(x, index):
        return roll(gather(x, index), 1, 0)

    def coefs(ref, ghosts, strip_ghosts):
        out = []
        ek, es, eu = (edges(tile(ref, 18 + f)) for f in (3, 4, 1))
        for l in range(LEVELS):
            u, v, k, s = (field(ref, f, l) for f in (2, 3, 4, 5))
            ke, kw = beside(k, ek, l)
            se, sw = beside(s, es, l)
            uw = beside(u, eu, l)[1]
            gs, gk = ghosts[l]
            out.append(coefficients(k, s, u, v, north(k, gk), ke, below(k), kw, north(s, gs), se, below(s), sw, uw, below(v)))
        u, v, k, s = (tile(ref, 18 + f) for f in (1, 2, 3, 4))
        gs, gk = strip_ghosts
        out.append(
            coefficients(
                k, s, u, v, north(k, gk), roll(k, -1), below(k), roll(k, 1), north(s, gs), roll(s, -1), below(s), roll(s, 1),
                roll(u, 1), below(v),
            )
        )
        return out

    def advance(c, q, strip, ghosts, strip_ghost):
        edge = edges(strip)
        out = []
        for j in range(6):
            e, w = beside(q[j], edge, j)
            out.append(stencil(c[j % 3], q[j], e, w, north(q[j], ghosts[j]), below(q[j])))
        new = stencil(c[3], strip, roll(strip, -1), roll(strip, 1), north(strip, strip_ghost), below(strip))
        return out, new

    zero = jnp.zeros((8, COLS), jnp.float32)
    d0 = [tile(d_ref, j) for j in range(6)]
    p0 = [tile(p_ref, j) for j in range(6)]
    static = [(fold(field(d_ref, 5, l), index_p), fold(field(d_ref, 4, l), index_p)) for l in range(LEVELS)]
    cp = coefs(p_ref, static, (outer(1), outer(2)))
    cd = coefs(d_ref, [(zero, zero)] * 3, (zero, zero))
    d1, _ = advance(cd, d0, tile(d_ref, 18), [zero] * 6, zero)
    p1, strip = advance(cp, p0, tile(p_ref, 18), [fold(x, index_p) for x in d0], outer(0))
    p2, strip = advance(cp, p1, strip, [fold(x, index_p) for x in d1], zero)
    p3, _ = advance(cp, p2, strip, [zero] * 6, zero)
    for j in range(6):
        l = j % 3
        values = [p0[j], p1[j], p2[j], p3[j], field(p_ref, 5, l), field(p_ref, 4, l)]
        out = zero
        for i, x in enumerate(values):
            out = jnp.where(row == i, roll(gather(x, index_d), i - 6, 0), out)
        gx_ref[pl.ds(8 * j, 8), :] = out
        gy_ref[pl.ds(8 * j, 8), :] = out
    tracers, coefs = (halo_tile(a_ref, b_ref, PACKED + n) for n in range(2))
    east, west = edge_message(tracers, coefs)
    gx_ref[pl.ds(GHOST_ROWS, 8), :] = jnp.where(odd, west, east)
    gy_ref[pl.ds(GHOST_ROWS, 8), :] = jnp.where(odd, east, west)


def ghosts(partner, own, xr, yr, ar, br):
    return pl.pallas_call(
        ghost_kernel,
        out_shape=(jax.ShapeDtypeStruct((GHOST_ROWS + 8, COLS), jnp.float32),) * 2,
        in_specs=vmem(6),
        out_specs=tuple(vmem(2)),
        compiler_params=PARAMS,
        name="ghost",
    )(partner, own, xr, yr, ar, br)


def coef_block(load, store):
    ku, ks, kk = (load(f, 4, 0) for f in (0, 3, 2))
    for l in range(4):
        u, v, k, s = (load(f, l, 0) for f in range(4))
        if l < 3:
            ke, kw = beside(k, kk, l)
            se, sw = beside(s, ks, l)
            uw = beside(u, ku, l)[1]
        else:
            ke, kw, se, sw, uw = roll(k, -1), roll(k, 1), roll(s, -1), roll(s, 1), roll(u, 1)
        out = coefficients(
            k, s, u, v, load(2, l, 1), ke, load(2, l, -1), kw, load(3, l, 1), se, load(3, l, -1), sw, uw, load(1, l, -1)
        )
        for n in range(5):
            store(n, l, out[n])


def advance(load, c, last):
    edge = load(7, 0)
    out = []
    for j in range(6):
        q = load(j, 0)
        e, w = beside(q, edge, j)
        out.append(stencil([c(n, j % 3) for n in range(5)], q, e, w, load(j, 1), load(j, -1)))
    if not last:
        strip = load(6, 0)
        strip_c = [c(n, 3) for n in range(5)]
        new = stencil(strip_c, strip, roll(strip, -1), roll(strip, 1), load(6, 1), load(6, -1))
        out += [new, edges(new)]
    return out


def outputs(out, sea, store):
    for l in range(LEVELS):
        heat, salt = out[l], out[3 + l]
        dens = sea(l) * (-0.2 * heat * (1.0 + 0.05 * heat) + 0.8 * salt - 0.01 * heat * salt)
        for n, x in enumerate((heat, salt, dens)):
            store(n, l, x)


def eight(r):
    return pl.ds(pl.multiple_of(r, 8), 8)


def coef_kernel(fields, pt_ref, pc_ref, xr_ref, yr_ref, strip_ref, edge_ref, coef):
    odd = lax.rem(lax.axis_index("lon"), 2) == 1

    def fill(i, carry):
        src = eight(i * 8)
        x, y = xr_ref[src, :], yr_ref[src, :]
        mw, me = jnp.where(odd, x, y), jnp.where(odd, y, x)
        for n, part in enumerate(strips(pt_ref[src, :], pc_ref[src, :], mw, me)):
            strip_ref[n, eight(i * 8 + BASE), :] = part
            if n != 2:
                edge_ref[n, eight(i * 8 + BASE), :] = edges(part)
        return carry

    lax.fori_loop(0, ROWS // 8, fill, 0, unroll=UNROLL)

    def block(i, carry):
        r = i * 8 + BASE

        def load(f, l, shift):
            rows = pl.ds(r + shift, 8)
            if l == 4:
                return edge_ref[1 + f, rows, :]
            return strip_ref[1 + f, rows, :] if l == 3 else fields[3 * f + l, rows, :]

        def store(n, l, x):
            coef[4 * n + l, eight(r), :] = x

        coef_block(load, store)
        return carry

    lax.fori_loop(0, ROWS // 8, block, 0, unroll=4)


def coefs_of(fields, pt, pc, xr, yr):
    def ext(n):
        return jax.ShapeDtypeStruct((n, EXT, COLS), jnp.float32)

    return pl.pallas_call(
        coef_kernel,
        out_shape=(ext(5), ext(5), ext(20)),
        in_specs=vmem(5),
        out_specs=tuple(vmem(3)),
        compiler_params=PARAMS,
        cost_estimate=pl.CostEstimate(flops=1000, bytes_accessed=1000, transcendentals=0),
        name="coefs",
    )(fields, pt, pc, xr, yr)


def steps_kernel(q_ref, fields, strip_ref, edge_ref, coef, heat_ref, salt_ref, dens_ref, qa, qb):
    results = (heat_ref, salt_ref, dens_ref)

    def loader(src, r):
        def load(j, shift):
            rows = pl.ds(r + shift, 8)
            if src is not None:
                return src[j, rows, :]
            return q_ref[j, rows, :] if j < 6 else (strip_ref, edge_ref)[j - 6][0, rows, :]

        return load

    def coefficient(r):
        return lambda n, l: coef[4 * n + l, eight(r), :]

    for src, dst in ((None, qa), (qa, qb), (qb, qa)):

        def block(i, carry):
            r = i * 8 + BASE
            for j, x in enumerate(advance(loader(src, r), coefficient(r), False)):
                dst[j, eight(r), :] = x
            return carry

        lax.fori_loop(0, ROWS // 8, block, 0, unroll=UNROLL)

    def final(i, carry):
        r = i * 8 + BASE
        rows = eight(i * 8)

        def store(n, l, x):
            results[n][l, rows, :] = x

        outputs(advance(loader(qa, r), coefficient(r), True), lambda l: fields[9 + l, eight(r), :], store)
        return carry

    lax.fori_loop(0, ROWS // 8, final, 0, unroll=UNROLL)


def inner_steps(q, fields, strip, edge, coef):
    out = jax.ShapeDtypeStruct((LEVELS, ROWS, COLS), jnp.float32)
    return pl.pallas_call(
        steps_kernel,
        out_shape=(out, out, out),
        in_specs=vmem(5),
        out_specs=tuple(vmem(3)),
        scratch_shapes=[pltpu.VMEM((8, EXT, COLS), jnp.float32)] * 2,
        compiler_params=PARAMS,
        cost_estimate=pl.CostEstimate(flops=1000, bytes_accessed=1000, transcendentals=0),
        name="steps",
    )(q, fields, strip, edge, coef)


ZONE = 64
SHIFT = NORTH - 48
SOUTH_BLOCKS = (8, 16, 24)
NORTH_BLOCKS = (32, 40, 48)


def zone_kernel(q_ref, fields, strip_ref, a_ref, b_ref, g_ref, gx_ref, gy_ref, *rest):
    h_out, s_out, d_out, *scratch = rest[3:]
    zq, zr, zf, zc, patch, sems = scratch
    odd = lax.rem(lax.axis_index("lon"), 2) == 1
    at_top = lax.axis_index("lat") == LAT - 1
    lane = iota(1)

    def place(j):
        if j < 6:
            return zq, j, q_ref, j
        if j < 18:
            return zf, 4 * ((j - 6) // 3) + j % 3, fields, j - 6
        if j == 18:
            return zq, 6, strip_ref, 0
        return zf, 4 * (j - 19) + 3, strip_ref, j - 18

    x, y = gx_ref[pl.ds(GHOST_ROWS, 8), :], gy_ref[pl.ds(GHOST_ROWS, 8), :]
    packed = [halo_tile(a_ref, b_ref, PACKED + n) for n in range(2)]
    halo = [halo_tile(a_ref, b_ref, j) for j in range(18)]
    halo += strips(*packed, jnp.where(odd, x, y), jnp.where(odd, y, x))
    for j in range(TILES):
        ref, n, src, m = place(j)
        ref[n, pl.ds(BASE, 16), :] = src[m, pl.ds(BASE, 16), :]
        ref[n, pl.ds(32, 16), :] = src[m, pl.ds(NORTH - 16, 16), :]
        ref[n, pl.ds(BASE - 4, 4), :] = halo[j][0:4]
        ref[n, pl.ds(48, 4), :] = halo[j][4:8]

    own = [g_ref[pl.ds(8 * j, 8), :] for j in range(6)]
    strip = jnp.zeros((8, COLS), jnp.float32)
    for j in range(6):
        x, y = gx_ref[pl.ds(8 * j, 8), :], gy_ref[pl.ds(8 * j, 8), :]
        west, east = jnp.where(odd, x, y), jnp.where(odd, y, x)
        strip = jnp.where((lane >> 3) == j, roll(jnp.where(lane >= COLS - 4, west, own[j]), 8 * j + 4), strip)
        strip = jnp.where((lane >> 3) == j + 6, roll(jnp.where(lane < 4, east, own[j]), 8 * j + 52), strip)

    ghost = pl.ds(48, 1)

    def put(ref, s):
        @pl.when(at_top)
        def _():
            for j in range(6):
                ref[j, ghost, :] = own[j][s : s + 1, :]
            ref[6, ghost, :] = strip[s : s + 1, :]

    put(zq, 0)

    @pl.when(at_top)
    def _():
        for f, s in ((3, 4), (2, 5)):
            for l in range(LEVELS):
                zf[4 * f + l, ghost, :] = own[l][s : s + 1, :]
            zf[4 * f + 3, ghost, :] = strip[s : s + 1, :]

    for r in SOUTH_BLOCKS + NORTH_BLOCKS:

        def load(f, l, shift):
            return zf[4 * f + l, pl.ds(r + shift, 8), :]

        def store(n, l, x):
            zc[4 * n + l, pl.ds(r, 8), :] = x

        def with_edges(f, l, shift):
            return edges(load(f, 3, shift)) if l == 4 else load(f, l, shift)

        coef_block(with_edges, store)

    def loader(src, r):
        def load(j, shift):
            return edges(src[6, pl.ds(r, 8), :]) if j == 7 else src[j, pl.ds(r + shift, 8), :]

        return load

    def coefficient(r):
        return lambda n, l: zc[4 * n + l, pl.ds(r, 8), :]

    for s, (src, dst) in enumerate(((zq, zr), (zr, zq), (zq, zr))):
        for r in SOUTH_BLOCKS + NORTH_BLOCKS:
            out = advance(loader(src, r), coefficient(r), False)
            for j, x in enumerate(out[:7]):
                dst[j, pl.ds(r, 8), :] = x
        put(dst, s + 1)

    copies = []
    for z, (r, row) in enumerate(((16, 0), (40, ROWS - 8))):

        def store(n, l, x):
            patch[2 * n + z, l, :, :] = x

        out = advance(loader(zr, r), coefficient(r), True)
        outputs(out, lambda l: zf[12 + l, pl.ds(r, 8), :], store)
        for n, ref in enumerate((h_out, s_out, d_out)):
            copy = pltpu.make_async_copy(patch.at[2 * n + z], ref.at[:, pl.ds(row, 8), :], sems.at[2 * n + z])
            copy.start()
            copies.append(copy)
    for copy in copies:
        copy.wait()


def zones(q, fields, strip, a, b, g, gx, gy, *results):
    out = jax.ShapeDtypeStruct((LEVELS, ROWS, COLS), jnp.float32)
    anywhere = [pl.BlockSpec(memory_space=pl.ANY)] * 3
    return pl.pallas_call(
        zone_kernel,
        out_shape=(out, out, out),
        in_specs=vmem(8) + anywhere,
        out_specs=tuple(anywhere),
        scratch_shapes=[
            pltpu.VMEM((7, ZONE, COLS), jnp.float32),
            pltpu.VMEM((7, ZONE, COLS), jnp.float32),
            pltpu.VMEM((16, ZONE, COLS), jnp.float32),
            pltpu.VMEM((20, ZONE, COLS), jnp.float32),
            pltpu.VMEM((6, LEVELS, 8, COLS), jnp.float32),
            pltpu.SemaphoreType.DMA((6,)),
        ],
        input_output_aliases={8: 0, 9: 1, 10: 2},
        compiler_params=PARAMS,
        name="zones",
    )(q, fields, strip, a, b, g, gx, gy, *results)


def fold_exchange(message, rotation):
    routes = {r: (r - HOP * (r // HOP % 2), r // HOP % 2) for r in range(LON)}
    merged = LON - 2 * HOP + HOP - 1
    routes[merged] = (merged - 2 * HOP, 2)
    routes[LON - 1] = (merged - 2 * HOP, 3)
    bases = sorted({base for base, _ in routes.values()})
    index = functools.reduce(
        lambda found, r: jnp.where(rotation == r, bases.index(routes[r][0]), found), range(1, LON), jnp.int32(0)
    )
    hops = jnp.where(rotation == merged, 2, jnp.where(rotation == LON - 1, 3, rotation // HOP % 2))
    received = lax.switch(index, [functools.partial(swap, pairs=fold_pairs(r)) for r in bases], message)

    def hop(x, count):
        return swap(x, PAIR_HOP) if count == 0 else hop(swap(x, PAIR_HOP), count - 1)

    return lax.switch(hops, [lambda x: x] + [functools.partial(hop, count=n) for n in range(3)], received)


def on_device(t, s, u, v, k, w, seam):
    m = seam.reshape(1, COLS)
    rotation = (seam[0] // COLS + 1 + lax.axis_index("lon")) % LON
    xs, ys, pt, pc, q, fields = pack(t, s, u, v, k, w, m)
    a, b = edge_rows(q, fields, pt, pc)
    ar = swap(a, PAIR_A)
    br = swap(b, PAIR_B)
    xr = swap(xs, PAIR_X)
    yr = swap(ys, PAIR_Y)
    message = top_rows(q, fields, pt, pc, xs, xr, yr)
    message, ar, br = lax.optimization_barrier((message, ar, br))
    partner = fold_exchange(message, rotation)
    gx, gy = ghosts(partner, message, xr, yr, ar, br)
    gxr = swap(gx, PAIR_X)
    gyr = swap(gy, PAIR_Y)
    operands, _ = lax.optimization_barrier(((fields, pt, pc, xr, yr), gx))
    strip, edge, coef = coefs_of(*operands)
    results = inner_steps(q, fields, strip, edge, coef)
    return zones(q, fields, strip, ar, br, gx, gxr, gyr, *results)


def solution(mesh):
    block = P(None, "lat", "lon")
    return jax.shard_map(
        on_device,
        mesh=mesh,
        in_specs=(block,) * 6 + (P("lon"),),
        out_specs=(block,) * 3,
        check_vma=False,
    )
```

```python
import functools

import jax
import jax.numpy as jnp
from jax import lax
from jax.experimental import pallas as pl
from jax.experimental.pallas import tpu as pltpu
from jax.sharding import PartitionSpec as P

STEPS = 4
LEVELS = 3
ROWS = 256
COLS = 128
LON = 64
LAT = 4
AXES = ("lon", "lat")
HOP = 8

BASE = 16
NORTH = BASE + ROWS
EXT = 288

TILES = 23
UNROLL = 8
GROUP = 4

SEAM = 5 * TILES + 3
FOLD_ROWS = 128
PACKED = 18
ROW_ROWS = 4 * 20
GHOST_ROWS = 48


def flat(lon, lat):
    return (lon % LON) * LAT + lat


def lon_pairs(partner):
    return [(flat(i, a), flat(partner(i), a)) for i in range(LON) for a in range(LAT)]


PAIR_X = lon_pairs(lambda i: i ^ 1)
PAIR_Y = lon_pairs(lambda i: ((i - 1) ^ 1) + 1)
PAIR_A = [(flat(i, a), flat(i, a ^ 1)) for i in range(LON) for a in range(LAT)]
PAIR_B = [(flat(i, a), flat(i, 3 - a)) for i in range(LON) for a in (1, 2)]


PAIR_HOP = [(flat(i, LAT - 1), flat(i + HOP, LAT - 1)) for i in range(LON)]


def fold_pairs(r):
    return [(flat(i, LAT - 1), flat(r - 1 - i, LAT - 1)) for i in range(LON)]


def swap(x, pairs):
    return lax.ppermute(x, AXES, pairs)


def iota(axis):
    return lax.broadcasted_iota(jnp.int32, (8, COLS), axis)


def roll(x, shift, axis=1):
    return pltpu.roll(x, shift % x.shape[axis], axis)


def sea_of(x):
    return x.astype(jnp.float32)


def vmem(n):
    return [pl.BlockSpec(memory_space=pltpu.VMEM)] * n


PARAMS = pltpu.CompilerParams(vmem_limit_bytes=32 << 20)


def pack_kernel(t_hbm, s_hbm, u_hbm, v_hbm, k_hbm, w_hbm, m_hbm, ys_ref, xs_ref, pt_ref, pc_ref, q_ref, f_ref, w_ref, m_ref, sems):
    odd = lax.rem(lax.axis_index("lon"), 2) == 1
    group = iota(1) >> 3
    own = pl.ds(BASE, ROWS)

    def target(n):
        if n >= 5:
            return (w_ref, m_ref)[n - 5]
        ref = q_ref if n < 2 else f_ref
        return ref.at[pl.ds(3 * (n if n < 2 else n - 2), LEVELS), own, :]

    copies = [
        pltpu.make_async_copy(src, target(n), sems.at[n])
        for n, src in enumerate((t_hbm, s_hbm, u_hbm, v_hbm, k_hbm, w_hbm, m_hbm))
    ]
    for copy in copies:
        copy.start()

    def gathered(ref, count, rows):
        out = jnp.zeros((8, COLS), jnp.float32)
        for j in range(count):
            out = jnp.where(group == j, roll(ref[j, rows, :], 4 + 8 * j), out)
        return out

    def tracer_block(i, carry):
        rows = pl.ds(pl.multiple_of(i * 8 + BASE, 8), 8)
        pt_ref[pl.ds(pl.multiple_of(i * 8, 8), 8), :] = gathered(q_ref, 6, rows)
        return carry

    def coef_block(i, carry):
        rows = pl.ds(pl.multiple_of(i * 8, 8), 8)
        here = pl.ds(pl.multiple_of(i * 8 + BASE, 8), 8)
        for l in range(LEVELS):
            f_ref[9 + l, here, :] = sea_of(w_ref[l, rows, :])
        tracers = pt_ref[rows, :]
        coefs = gathered(f_ref, 12, here)
        pc_ref[rows, :] = coefs
        east, west = edge_message(tracers, coefs)
        xs_ref[rows, :] = jnp.where(odd, west, east)
        ys_ref[rows, :] = jnp.where(odd, east, west)
        return carry

    copies[0].wait()
    copies[1].wait()
    lax.fori_loop(0, ROWS // 8, tracer_block, 0, unroll=8)
    for copy in copies[2:]:
        copy.wait()
    lax.fori_loop(0, ROWS // 8, coef_block, 0, unroll=4)
    second = pl.ds(BASE + ROWS - 2, 1)
    for out in (xs_ref, ys_ref):
        for n in range(6):
            out[pl.ds(ROWS + n, 1), :] = q_ref[n, second, :]
        for l in range(LEVELS):
            out[pl.ds(ROWS + 6 + l, 1), :] = f_ref[9 + l, second, :]
            out[pl.ds(ROWS + 9 + l, 1), :] = f_ref[6 + l, second, :]
        out[pl.ds(ROWS + 12, 1), :] = m_ref[...].astype(jnp.float32)
        out[pl.ds(ROWS + 13, 3), :] = jnp.zeros((3, COLS), jnp.float32)


def pack(t, s, u, v, k, w, m):
    edge = jax.ShapeDtypeStruct((ROWS + 16, COLS), jnp.float32)
    own = jax.ShapeDtypeStruct((ROWS, COLS), jnp.float32)
    return pl.pallas_call(
        pack_kernel,
        out_shape=(
            edge,
            edge,
            own,
            own,
            jax.ShapeDtypeStruct((6, EXT, COLS), jnp.float32),
            jax.ShapeDtypeStruct((12, EXT, COLS), jnp.float32),
        ),
        in_specs=[pl.BlockSpec(memory_space=pltpu.HBM)] * 7,
        out_specs=tuple(vmem(6)),
        scratch_shapes=[
            pltpu.VMEM((LEVELS, ROWS, COLS), jnp.int32),
            pltpu.VMEM((1, COLS), jnp.int32),
            pltpu.SemaphoreType.DMA((7,)),
        ],
        compiler_params=PARAMS,
        name="pack",
    )(*(pltpu.with_memory_space_constraint(x, pltpu.HBM) for x in (t, s, u, v, k, w, m)))


def rows_kernel(q_ref, fields, pt_ref, pc_ref, a_ref, b_ref):
    odd_lat = lax.rem(lax.axis_index("lat"), 2) == 1
    for j in range(20):
        if j < 18:
            ref, n = (q_ref, j) if j < 6 else (fields, j - 6)
            down, up = ref[n, pl.ds(BASE, 8), :][0:4], ref[n, pl.ds(NORTH - 8, 8), :][4:8]
        else:
            ref = (pt_ref, pc_ref)[j - 18]
            down, up = ref[pl.ds(0, 8), :][0:4], ref[pl.ds(ROWS - 8, 8), :][4:8]
        a_ref[pl.ds(4 * j, 4), :] = jnp.where(odd_lat, down, up)
        b_ref[pl.ds(4 * j, 4), :] = jnp.where(odd_lat, up, down)


def edge_rows(q, fields, pt, pc):
    return pl.pallas_call(
        rows_kernel,
        out_shape=(jax.ShapeDtypeStruct((ROW_ROWS, COLS), jnp.float32),) * 2,
        in_specs=vmem(4),
        out_specs=tuple(vmem(2)),
        compiler_params=PARAMS,
        name="rows",
    )(q, fields, pt, pc)


def edge_message(tracers, coefs):
    low = (iota(1) & 7) < 4
    return jnp.where(low, coefs, roll(tracers, 4)), jnp.where(low, roll(tracers, -4), coefs)


def halo_tile(a_ref, b_ref, j):
    odd_lat = lax.rem(lax.axis_index("lat"), 2) == 1
    a, b = a_ref[pl.ds(4 * j, 4), :], b_ref[pl.ds(4 * j, 4), :]
    return jnp.concatenate([jnp.where(odd_lat, a, b), jnp.where(odd_lat, b, a)], axis=0)


def strips(pt, pc, mw, me):
    lane = iota(1)
    low = (lane & 7) < 4
    wt = jnp.where(low, roll(mw, -4), pt)
    et = jnp.where(low, pt, roll(me, 4))
    wc = jnp.where(low, mw, pc)
    ec = jnp.where(low, pc, me)
    out = [jnp.where(lane < 48, wt, roll(et, 48))]
    for f in range(4):
        west = jnp.where(lane < 24, roll(wc, -24 * f), roll(wc, 24 - 24 * f))
        east = jnp.where(lane < 72, roll(ec, 48 - 24 * f), roll(ec, 72 - 24 * f))
        out.append(jnp.where(lane < 48, west, east))
    return out


def top_kernel(q_ref, fields, pt_ref, pc_ref, xs_ref, xr_ref, yr_ref, f_ref):
    odd = lax.rem(lax.axis_index("lon"), 2) == 1
    rows = pl.ds(ROWS - 8, 8)
    here = pl.ds(NORTH - 8, 8)
    x, y = xr_ref[rows, :], yr_ref[rows, :]
    mw, me = jnp.where(odd, x, y), jnp.where(odd, y, x)
    tiles = [q_ref[n, here, :] for n in range(6)] + [fields[n, here, :] for n in range(12)]
    tiles += strips(pt_ref[rows, :], pc_ref[rows, :], mw, me)
    f_ref[pl.ds(0, 3), :] = jnp.zeros((3, COLS), jnp.float32)
    for j in range(TILES):
        f_ref[pl.ds(5 * j + 3, 5), :] = tiles[j][3:8, :]
    x, y = xr_ref[pl.ds(ROWS + 8, 8), :], yr_ref[pl.ds(ROWS + 8, 8), :]
    ew, ee = jnp.where(odd, x, y), jnp.where(odd, y, x)
    f_ref[pl.ds(SEAM, 1), :] = xs_ref[pl.ds(ROWS + 12, 1), :]
    f_ref[pl.ds(SEAM + 1, 1), :] = ew[4:5, :]
    f_ref[pl.ds(SEAM + 2, 1), :] = ee[4:5, :]
    f_ref[pl.ds(SEAM + 3, FOLD_ROWS - SEAM - 3), :] = jnp.zeros((FOLD_ROWS - SEAM - 3, COLS), jnp.float32)


def top_rows(q, fields, pt, pc, xs, xr, yr):
    return pl.pallas_call(
        top_kernel,
        out_shape=jax.ShapeDtypeStruct((FOLD_ROWS, COLS), jnp.float32),
        in_specs=vmem(7),
        out_specs=vmem(1)[0],
        compiler_params=PARAMS,
        name="top",
    )(q, fields, pt, pc, xs, xr, yr)


def coefficients(k, s, u, v, kn, ke, ks, kw, sn, se, ss, sw, uw, vs):
    zero = jnp.zeros_like(k)
    fe, fw, fn, fs = 0.5 * (k + ke), 0.5 * (kw + k), 0.5 * (k + kn), 0.5 * (ks + k)
    oe, ow, on, os = s * se, sw * s, s * sn, ss * s
    ae, be = oe * (jnp.maximum(u, zero) + fe), oe * (jnp.minimum(u, zero) - fe)
    aw, bw = ow * (jnp.maximum(uw, zero) + fw), ow * (jnp.minimum(uw, zero) - fw)
    an, bn = on * (jnp.maximum(v, zero) + fn), on * (jnp.minimum(v, zero) - fn)
    a_s, bs = os * (jnp.maximum(vs, zero) + fs), os * (jnp.minimum(vs, zero) - fs)
    centre = s - (ae - bw) - (an - bs)
    return centre, -be, aw, -bn, a_s


def stencil(c, q, e, w, n, s):
    return c[0] * q + c[1] * e + c[2] * w + c[3] * n + c[4] * s


def edges(strip):
    return jnp.where((iota(1) & 7) == 3, strip, roll(strip, -50))


def beside_strip(x, strip, j):
    lane = iota(1)
    west, east = roll(strip, -(8 * j + 3)), roll(strip, -(8 * j + 53))
    return jnp.where(lane == COLS - 1, east, roll(x, -1)), jnp.where(lane == 0, west, roll(x, 1))


def beside(x, edge, j):
    lane = iota(1)
    z = roll(edge, -(8 * j + 3))
    return jnp.where(lane == COLS - 1, z, roll(x, -1)), jnp.where(lane == 0, z, roll(x, 1))


def gather(x, index):
    return jnp.take_along_axis(x, index, axis=1)


def ghost_kernel(p_ref, d_ref, xe_ref, ye_ref, a_ref, b_ref, gy_ref, gx_ref):
    odd = lax.rem(lax.axis_index("lon"), 2) == 1
    row, lane = iota(0), iota(1)
    top = row == 7

    def tile(ref, j):
        return ref[pl.ds(5 * j, 8), :]

    def spread(index_row):
        return jnp.broadcast_to(index_row.astype(jnp.int32) & (COLS - 1), (8, COLS))

    index_d = spread(d_ref[pl.ds(SEAM, 1), :])
    index_p = spread(p_ref[pl.ds(SEAM, 1), :])
    index_pw = spread(p_ref[pl.ds(SEAM + 1, 1), :])
    index_pe = spread(p_ref[pl.ds(SEAM + 2, 1), :])
    xe0, ye0 = xe_ref[pl.ds(ROWS, 8), :], ye_ref[pl.ds(ROWS, 8), :]
    xe1, ye1 = xe_ref[pl.ds(ROWS + 8, 8), :], ye_ref[pl.ds(ROWS + 8, 8), :]
    east = [gather(jnp.where(odd, y, x), index_pw) for x, y in ((xe0, ye0), (xe1, ye1))]
    west = [gather(jnp.where(odd, x, y), index_pe) for x, y in ((xe0, ye0), (xe1, ye1))]

    def outer(kind):
        out = jnp.zeros((8, COLS), jnp.float32)
        for j in range(6):
            n = (j, 6 + j % 3, 9 + j % 3)[kind]
            w = jnp.broadcast_to(east[n // 8][n % 8 : n % 8 + 1, :], (8, COLS))
            e = jnp.broadcast_to(west[n // 8][n % 8 : n % 8 + 1, :], (8, COLS))
            out = jnp.where((lane >> 3) == j, roll(w, 8 * j + 4), out)
            out = jnp.where((lane >> 3) == j + 6, roll(e, 8 * j + 52), out)
        return out

    def north(x, ghost):
        return jnp.where(top, ghost, roll(x, -1, 0))

    def below(x):
        return roll(x, 1, 0)

    def field(ref, f, l):
        return tile(ref, 3 * f + l)

    def fold(x, index):
        return roll(gather(x, index), 1, 0)

    def coefs(ref, ghosts, strip_ghosts):
        out = []
        ek, es, eu = (tile(ref, 18 + f) for f in (3, 4, 1))
        for l in range(LEVELS):
            u, v, k, s = (field(ref, f, l) for f in (2, 3, 4, 5))
            ke, kw = beside_strip(k, ek, l)
            se, sw = beside_strip(s, es, l)
            uw = beside_strip(u, eu, l)[1]
            gs, gk = ghosts[l]
            out.append(coefficients(k, s, u, v, north(k, gk), ke, below(k), kw, north(s, gs), se, below(s), sw, uw, below(v)))
        u, v, k, s = (tile(ref, 18 + f) for f in (1, 2, 3, 4))
        gs, gk = strip_ghosts
        out.append(
            coefficients(
                k, s, u, v, north(k, gk), roll(k, -1), below(k), roll(k, 1), north(s, gs), roll(s, -1), below(s), roll(s, 1),
                roll(u, 1), below(v),
            )
        )
        return out

    def advance(c, q, strip, ghosts, strip_ghost):
        out = []
        for j in range(6):
            e, w = beside_strip(q[j], strip, j)
            out.append(stencil(c[j % 3], q[j], e, w, north(q[j], ghosts[j]), below(q[j])))
        new = stencil(c[3], strip, roll(strip, -1), roll(strip, 1), north(strip, strip_ghost), below(strip))
        return out, new

    zero = jnp.zeros((8, COLS), jnp.float32)
    d0 = [tile(d_ref, j) for j in range(6)]
    p0 = [tile(p_ref, j) for j in range(6)]
    static = [(fold(field(d_ref, 5, l), index_p), fold(field(d_ref, 4, l), index_p)) for l in range(LEVELS)]
    cp = coefs(p_ref, static, (outer(1), outer(2)))
    cd = coefs(d_ref, [(zero, zero)] * 3, (zero, zero))
    d1, _ = advance(cd, d0, tile(d_ref, 18), [zero] * 6, zero)
    p1, strip = advance(cp, p0, tile(p_ref, 18), [fold(x, index_p) for x in d0], outer(0))
    p2, strip = advance(cp, p1, strip, [fold(x, index_p) for x in d1], zero)
    p3, _ = advance(cp, p2, strip, [zero] * 6, zero)
    for j in range(6):
        l = j % 3
        values = [p0[j], p1[j], p2[j], p3[j], field(p_ref, 5, l), field(p_ref, 4, l)]
        out = zero
        for i, x in enumerate(values):
            out = jnp.where(row == i, roll(gather(x, index_d), i - 6, 0), out)
        gx_ref[pl.ds(8 * j, 8), :] = out
        gy_ref[pl.ds(8 * j, 8), :] = out
    tracers, coefs = (halo_tile(a_ref, b_ref, PACKED + n) for n in range(2))
    east, west = edge_message(tracers, coefs)
    gx_ref[pl.ds(GHOST_ROWS, 8), :] = jnp.where(odd, west, east)
    gy_ref[pl.ds(GHOST_ROWS, 8), :] = jnp.where(odd, east, west)


def ghosts(partner, own, xr, yr, ar, br):
    return pl.pallas_call(
        ghost_kernel,
        out_shape=(jax.ShapeDtypeStruct((GHOST_ROWS + 8, COLS), jnp.float32),) * 2,
        in_specs=vmem(6),
        out_specs=tuple(vmem(2)),
        compiler_params=PARAMS,
        name="ghost",
    )(partner, own, xr, yr, ar, br)


def coef_block(load, store, beside=beside):
    ku, ks, kk = (load(f, 4, 0) for f in (0, 3, 2))
    for l in range(4):
        u, v, k, s = (load(f, l, 0) for f in range(4))
        if l < 3:
            ke, kw = beside(k, kk, l)
            se, sw = beside(s, ks, l)
            uw = beside(u, ku, l)[1]
        else:
            ke, kw, se, sw, uw = roll(k, -1), roll(k, 1), roll(s, -1), roll(s, 1), roll(u, 1)
        out = coefficients(
            k, s, u, v, load(2, l, 1), ke, load(2, l, -1), kw, load(3, l, 1), se, load(3, l, -1), sw, uw, load(1, l, -1)
        )
        for n in range(5):
            store(n, l, out[n])


def advance(load, c, last, beside=beside):
    edge = load(7, 0)
    out = []
    for j in range(6):
        q = load(j, 0)
        e, w = beside(q, edge, j)
        out.append(stencil([c(n, j % 3) for n in range(5)], q, e, w, load(j, 1), load(j, -1)))
    if not last:
        strip = load(6, 0)
        strip_c = [c(n, 3) for n in range(5)]
        new = stencil(strip_c, strip, roll(strip, -1), roll(strip, 1), load(6, 1), load(6, -1))
        out += [new, edges(new)]
    return out


def outputs(out, sea, store):
    for l in range(LEVELS):
        heat, salt = out[l], out[3 + l]
        dens = sea(l) * (-0.2 * heat * (1.0 + 0.05 * heat) + 0.8 * salt - 0.01 * heat * salt)
        for n, x in enumerate((heat, salt, dens)):
            store(n, l, x)


def eight(r):
    return pl.ds(pl.multiple_of(r, 8), 8)


def coef_kernel(fields, pt_ref, pc_ref, xr_ref, yr_ref, strip_ref, edge_ref, coef):
    odd = lax.rem(lax.axis_index("lon"), 2) == 1

    def fill(i, carry):
        src = eight(i * 8)
        x, y = xr_ref[src, :], yr_ref[src, :]
        mw, me = jnp.where(odd, x, y), jnp.where(odd, y, x)
        for n, part in enumerate(strips(pt_ref[src, :], pc_ref[src, :], mw, me)):
            strip_ref[n, eight(i * 8 + BASE), :] = part
            if n != 2:
                edge_ref[n, eight(i * 8 + BASE), :] = edges(part)
        return carry

    lax.fori_loop(0, ROWS // 8, fill, 0, unroll=UNROLL)

    def block(i, carry):
        r = i * 8 + BASE

        def load(f, l, shift):
            rows = pl.ds(r + shift, 8)
            if l == 4:
                return edge_ref[1 + f, rows, :]
            return strip_ref[1 + f, rows, :] if l == 3 else fields[3 * f + l, rows, :]

        def store(n, l, x):
            coef[4 * n + l, eight(r), :] = x

        coef_block(load, store)
        return carry

    lax.fori_loop(0, ROWS // 8, block, 0, unroll=4)


def coefs_of(fields, pt, pc, xr, yr):
    def ext(n):
        return jax.ShapeDtypeStruct((n, EXT, COLS), jnp.float32)

    return pl.pallas_call(
        coef_kernel,
        out_shape=(ext(5), ext(5), ext(20)),
        in_specs=vmem(5),
        out_specs=tuple(vmem(3)),
        compiler_params=PARAMS,
        cost_estimate=pl.CostEstimate(flops=1000, bytes_accessed=1000, transcendentals=0),
        name="coefs",
    )(fields, pt, pc, xr, yr)


def steps_kernel(q_ref, fields, strip_ref, edge_ref, coef, heat_ref, salt_ref, dens_ref, qa, qb):
    results = (heat_ref, salt_ref, dens_ref)

    def loader(src, r):
        def load(j, shift):
            rows = pl.ds(r + shift, 8)
            if src is not None:
                return src[j, rows, :]
            return q_ref[j, rows, :] if j < 6 else (strip_ref, edge_ref)[j - 6][0, rows, :]

        return load

    def coefficient(r):
        return lambda n, l: coef[4 * n + l, eight(r), :]

    def groups(work):
        def body(k, carry):
            later = [work(8 * (GROUP * k + i) + BASE) for i in range(GROUP)]
            for stores in later:
                for ref, n, rows, x in stores:
                    ref[n, rows, :] = x
            return carry

        lax.fori_loop(0, ROWS // 8 // GROUP, body, 0)

    for src, dst in ((None, qa), (qa, qb), (qb, qa)):

        def block(r):
            return [(dst, j, eight(r), x) for j, x in enumerate(advance(loader(src, r), coefficient(r), False))]

        groups(block)

    def final(r):
        out = []

        def store(n, l, x):
            out.append((results[n], l, eight(r - BASE), x))

        outputs(advance(loader(qa, r), coefficient(r), True), lambda l: fields[9 + l, eight(r), :], store)
        return out

    groups(final)


def inner_steps(q, fields, strip, edge, coef):
    out = jax.ShapeDtypeStruct((LEVELS, ROWS, COLS), jnp.float32)
    return pl.pallas_call(
        steps_kernel,
        out_shape=(out, out, out),
        in_specs=vmem(5),
        out_specs=tuple(vmem(3)),
        scratch_shapes=[pltpu.VMEM((8, EXT, COLS), jnp.float32)] * 2,
        compiler_params=PARAMS,
        cost_estimate=pl.CostEstimate(flops=1000, bytes_accessed=1000, transcendentals=0),
        name="steps",
    )(q, fields, strip, edge, coef)


ZONE = 64
SHIFT = NORTH - 48
SOUTH_BLOCKS = (8, 16)
NORTH_BLOCKS = (40, 48)


def zone_kernel(q_ref, fields, strip_ref, a_ref, b_ref, g_ref, gx_ref, gy_ref, *rest):
    h_out, s_out, d_out, *scratch = rest[3:]
    zq, zr, zf, zc, patch, sems = scratch
    odd = lax.rem(lax.axis_index("lon"), 2) == 1
    at_top = lax.axis_index("lat") == LAT - 1
    lane = iota(1)

    def place(j):
        if j < 6:
            return zq, j, q_ref, j
        if j < 18:
            return zf, 4 * ((j - 6) // 3) + j % 3, fields, j - 6
        if j == 18:
            return zq, 6, strip_ref, 0
        return zf, 4 * (j - 19) + 3, strip_ref, j - 18

    x, y = gx_ref[pl.ds(GHOST_ROWS, 8), :], gy_ref[pl.ds(GHOST_ROWS, 8), :]
    packed = [halo_tile(a_ref, b_ref, PACKED + n) for n in range(2)]
    halo = [halo_tile(a_ref, b_ref, j) for j in range(18)]
    halo += strips(*packed, jnp.where(odd, x, y), jnp.where(odd, y, x))
    for j in range(TILES):
        ref, n, src, m = place(j)
        ref[n, pl.ds(BASE, 16), :] = src[m, pl.ds(BASE, 16), :]
        ref[n, pl.ds(32, 16), :] = src[m, pl.ds(NORTH - 16, 16), :]
        ref[n, pl.ds(BASE - 4, 4), :] = halo[j][0:4]
        ref[n, pl.ds(48, 4), :] = halo[j][4:8]

    own = [g_ref[pl.ds(8 * j, 8), :] for j in range(6)]
    strip = jnp.zeros((8, COLS), jnp.float32)
    for j in range(6):
        x, y = gx_ref[pl.ds(8 * j, 8), :], gy_ref[pl.ds(8 * j, 8), :]
        west, east = jnp.where(odd, x, y), jnp.where(odd, y, x)
        strip = jnp.where((lane >> 3) == j, roll(jnp.where(lane >= COLS - 4, west, own[j]), 8 * j + 4), strip)
        strip = jnp.where((lane >> 3) == j + 6, roll(jnp.where(lane < 4, east, own[j]), 8 * j + 52), strip)

    ghost = pl.ds(48, 1)

    def put(ref, s):
        @pl.when(at_top)
        def _():
            for j in range(6):
                ref[j, ghost, :] = own[j][s : s + 1, :]
            ref[6, ghost, :] = strip[s : s + 1, :]

    put(zq, 0)

    @pl.when(at_top)
    def _():
        for f, s in ((3, 4), (2, 5)):
            for l in range(LEVELS):
                zf[4 * f + l, ghost, :] = own[l][s : s + 1, :]
            zf[4 * f + 3, ghost, :] = strip[s : s + 1, :]

    for r in SOUTH_BLOCKS + NORTH_BLOCKS:

        def load(f, l, shift):
            return zf[4 * f + l, pl.ds(r + shift, 8), :]

        def store(n, l, x):
            zc[4 * n + l, pl.ds(r, 8), :] = x

        coef_block(lambda f, l, shift: load(f, min(l, 3), shift), store, beside_strip)

    def loader(src, r):
        def load(j, shift):
            return src[min(j, 6), pl.ds(r + shift, 8), :]

        return load

    def coefficient(r):
        return lambda n, l: zc[4 * n + l, pl.ds(r, 8), :]

    for s, (src, dst) in enumerate(((zq, zr), (zr, zq), (zq, zr))):
        for r in SOUTH_BLOCKS + NORTH_BLOCKS:
            out = advance(loader(src, r), coefficient(r), False, beside_strip)
            for j, x in enumerate(out[:7]):
                dst[j, pl.ds(r, 8), :] = x
        put(dst, s + 1)

    copies = []
    for z, (r, row, part) in enumerate(((16, 0, 0), (40, ROWS - 4, 4))):

        def store(n, l, x):
            patch[2 * n + z, l, :, :] = x

        out = advance(loader(zr, r), coefficient(r), True, beside_strip)
        outputs(out, lambda l: zf[12 + l, pl.ds(r, 8), :], store)
        for n, ref in enumerate((h_out, s_out, d_out)):
            copy = pltpu.make_async_copy(patch.at[2 * n + z, :, pl.ds(part, 4), :], ref.at[:, pl.ds(row, 4), :], sems.at[2 * n + z])
            copy.start()
            copies.append(copy)
    for copy in copies:
        copy.wait()


def zones(q, fields, strip, a, b, g, gx, gy, *results):
    out = jax.ShapeDtypeStruct((LEVELS, ROWS, COLS), jnp.float32)
    anywhere = [pl.BlockSpec(memory_space=pl.ANY)] * 3
    return pl.pallas_call(
        zone_kernel,
        out_shape=(out, out, out),
        in_specs=vmem(8) + anywhere,
        out_specs=tuple(anywhere),
        scratch_shapes=[
            pltpu.VMEM((7, ZONE, COLS), jnp.float32),
            pltpu.VMEM((7, ZONE, COLS), jnp.float32),
            pltpu.VMEM((16, ZONE, COLS), jnp.float32),
            pltpu.VMEM((20, ZONE, COLS), jnp.float32),
            pltpu.VMEM((6, LEVELS, 8, COLS), jnp.float32),
            pltpu.SemaphoreType.DMA((6,)),
        ],
        input_output_aliases={8: 0, 9: 1, 10: 2},
        compiler_params=PARAMS,
        name="zones",
    )(q, fields, strip, a, b, g, gx, gy, *results)


def fold_exchange(message, rotation):
    patterns = [fold_pairs(r) for r in range(LON) if r // HOP % 2 == 0][:-1]
    index = ((rotation >> 4) << 3) + (rotation & 7)
    left_out = index == len(patterns)
    index = jnp.where(left_out, index - HOP, index)
    hops = ((rotation >> 3) & 1) + jnp.where(left_out, 2, 0)
    received = lax.switch(index, [functools.partial(swap, pairs=pairs) for pairs in patterns], message)

    def hop(x, count):
        return swap(x, PAIR_HOP) if count == 0 else hop(swap(x, PAIR_HOP), count - 1)

    return lax.switch(hops, [lambda x: x] + [functools.partial(hop, count=n) for n in range(3)], received)


def on_device(t, s, u, v, k, w, seam):
    m = seam.reshape(1, COLS)
    rotation = ((seam[0] >> 7) + 1 + lax.axis_index("lon")) & (LON - 1)
    ys, xs, pt, pc, q, fields = pack(t, s, u, v, k, w, m)
    a, b = edge_rows(q, fields, pt, pc)
    ar = swap(a, PAIR_A)
    br = swap(b, PAIR_B)
    xr = swap(xs, PAIR_X)
    yr = swap(ys, PAIR_Y)
    message = top_rows(q, fields, pt, pc, xs, xr, yr)
    message, ar, br = lax.optimization_barrier((message, ar, br))
    partner = fold_exchange(message, rotation)
    gy, gx = ghosts(partner, message, xr, yr, ar, br)
    gxr = swap(gx, PAIR_X)
    gyr = swap(gy, PAIR_Y)
    operands, _ = lax.optimization_barrier(((fields, pt, pc, xr, yr), gx))
    strip, edge, coef = coefs_of(*operands)
    results = inner_steps(q, fields, strip, edge, coef)
    return zones(q, fields, strip, ar, br, gx, gxr, gyr, *results)


def solution(mesh):
    block = P(None, "lat", "lon")
    return jax.shard_map(
        on_device,
        mesh=mesh,
        in_specs=(block,) * 6 + (P("lon"),),
        out_specs=(block,) * 3,
        check_vma=False,
    )
```

```python
import functools

import jax
import jax.numpy as jnp
from jax import lax
from jax.experimental import pallas as pl
from jax.experimental.pallas import tpu as pltpu
from jax.sharding import PartitionSpec as P

STEPS = 4
LEVELS = 3
ROWS = 256
COLS = 128
LON = 64
LAT = 4
AXES = ("lon", "lat")
HOP = 8

BASE = 16
NORTH = BASE + ROWS
EXT = 288

TILES = 23
UNROLL = 8
GROUP = 4
GROUPS = ROWS // 8 // GROUP
PARTS = 2

SEAM = 5 * TILES + 3
FOLD_ROWS = 128
PACKED = 18
BODY = 192
USED = 96
ROW_ROWS = 4 * 20
GHOST_ROWS = 48


def flat(lon, lat):
    return (lon % LON) * LAT + lat


def lon_pairs(partner):
    return [(flat(i, a), flat(partner(i), a)) for i in range(LON) for a in range(LAT)]


PAIR_X = lon_pairs(lambda i: i ^ 1)
PAIR_Y = lon_pairs(lambda i: ((i - 1) ^ 1) + 1)
PAIR_A = [(flat(i, a), flat(i, a ^ 1)) for i in range(LON) for a in range(LAT)]
PAIR_B = [(flat(i, a), flat(i, 3 - a)) for i in range(LON) for a in (1, 2)]


PAIR_HOP = [(flat(i, LAT - 1), flat(i + HOP, LAT - 1)) for i in range(LON)]


def fold_pairs(r):
    return [(flat(i, LAT - 1), flat(r - 1 - i, LAT - 1)) for i in range(LON)]


def swap(x, pairs):
    return lax.ppermute(x, AXES, pairs)


def iota(axis):
    return lax.broadcasted_iota(jnp.int32, (8, COLS), axis)


def roll(x, shift, axis=1):
    return pltpu.roll(x, shift % x.shape[axis], axis)


def sea_of(x):
    return x.astype(jnp.float32)


def vmem(n):
    return [pl.BlockSpec(memory_space=pltpu.VMEM)] * n


PARAMS = pltpu.CompilerParams(vmem_limit_bytes=32 << 20)


def pack_kernel(t_hbm, s_hbm, u_hbm, v_hbm, k_hbm, w_hbm, m_hbm, ys_ref, xs_ref, pt_ref, pc_ref, q_ref, f_ref, w_ref, m_ref, tail_ref, sems):
    odd = lax.rem(lax.axis_index("lon"), 2) == 1
    lane = iota(1)
    group = lane >> 3
    own = pl.ds(BASE, ROWS)

    def target(n):
        if n >= 5:
            return (w_ref, m_ref)[n - 5]
        ref = q_ref if n < 2 else f_ref
        return ref.at[pl.ds(3 * (n if n < 2 else n - 2), LEVELS), own, :]

    copies = [
        pltpu.make_async_copy(src, target(n), sems.at[n])
        for n, src in enumerate((t_hbm, s_hbm, u_hbm, v_hbm, k_hbm, w_hbm, m_hbm))
    ]
    for copy in copies:
        copy.start()

    def gathered(ref, count, rows):
        out = jnp.zeros((8, COLS), jnp.float32)
        for j in range(count):
            out = jnp.where(group == j, roll(ref[j, rows, :], 4 + 8 * j), out)
        return out

    def tracer_block(i, carry):
        rows = pl.ds(pl.multiple_of(i * 8 + BASE, 8), 8)
        pt_ref[pl.ds(pl.multiple_of(i * 8, 8), 8), :] = gathered(q_ref, 6, rows)
        return carry

    def messages(i):
        rows = eight(i * 8)
        here = eight(i * 8 + BASE)
        for l in range(LEVELS):
            f_ref[9 + l, here, :] = sea_of(w_ref[l, rows, :])
        tracers = pt_ref[rows, :]
        coefs = gathered(f_ref, 12, here)
        pc_ref[rows, :] = coefs
        east, west = edge_message(tracers, coefs)
        return jnp.where(odd, west, east), jnp.where(odd, east, west)

    def last_block(i, carry):
        for n, x in enumerate(messages(i + BODY // 8)):
            tail_ref[n, eight(i * 8), :] = x
        return carry

    def coef_block(third):
        def block(i, carry):
            for n, (ref, x) in enumerate(zip((xs_ref, ys_ref), messages(8 * third + i))):
                rest = roll(tail_ref[n, eight(i * 8), :], USED - 32 * third)
                ref[eight(64 * third + i * 8), :] = jnp.where(lane < USED, x, rest)
            return carry

        return block

    copies[0].wait()
    copies[1].wait()
    lax.fori_loop(0, ROWS // 8, tracer_block, 0, unroll=8)
    for copy in copies[2:]:
        copy.wait()
    lax.fori_loop(0, 8, last_block, 0, unroll=UNROLL)
    for third in range(3):
        lax.fori_loop(0, 8, coef_block(third), 0, unroll=UNROLL)
    second = pl.ds(BASE + ROWS - 2, 1)
    for out in (xs_ref, ys_ref):
        for n in range(6):
            out[pl.ds(BODY + n, 1), :] = q_ref[n, second, :]
        for l in range(LEVELS):
            out[pl.ds(BODY + 6 + l, 1), :] = f_ref[9 + l, second, :]
            out[pl.ds(BODY + 9 + l, 1), :] = f_ref[6 + l, second, :]
        out[pl.ds(BODY + 12, 1), :] = m_ref[...].astype(jnp.float32)
        out[pl.ds(BODY + 13, 3), :] = jnp.zeros((3, COLS), jnp.float32)


def pack(t, s, u, v, k, w, m):
    edge = jax.ShapeDtypeStruct((BODY + 16, COLS), jnp.float32)
    own = jax.ShapeDtypeStruct((ROWS, COLS), jnp.float32)
    return pl.pallas_call(
        pack_kernel,
        out_shape=(
            edge,
            edge,
            own,
            own,
            jax.ShapeDtypeStruct((6, EXT, COLS), jnp.float32),
            jax.ShapeDtypeStruct((12, EXT, COLS), jnp.float32),
        ),
        in_specs=[pl.BlockSpec(memory_space=pltpu.HBM)] * 7,
        out_specs=tuple(vmem(6)),
        scratch_shapes=[
            pltpu.VMEM((LEVELS, ROWS, COLS), jnp.int32),
            pltpu.VMEM((1, COLS), jnp.int32),
            pltpu.VMEM((2, ROWS - BODY, COLS), jnp.float32),
            pltpu.SemaphoreType.DMA((7,)),
        ],
        compiler_params=PARAMS,
        name="pack",
    )(*(pltpu.with_memory_space_constraint(x, pltpu.HBM) for x in (t, s, u, v, k, w, m)))


def rows_kernel(q_ref, fields, pt_ref, pc_ref, a_ref, b_ref):
    odd_lat = lax.rem(lax.axis_index("lat"), 2) == 1
    for j in range(20):
        if j < 18:
            ref, n = (q_ref, j) if j < 6 else (fields, j - 6)
            down, up = ref[n, pl.ds(BASE, 8), :][0:4], ref[n, pl.ds(NORTH - 8, 8), :][4:8]
        else:
            ref = (pt_ref, pc_ref)[j - 18]
            down, up = ref[pl.ds(0, 8), :][0:4], ref[pl.ds(ROWS - 8, 8), :][4:8]
        a_ref[pl.ds(4 * j, 4), :] = jnp.where(odd_lat, down, up)
        b_ref[pl.ds(4 * j, 4), :] = jnp.where(odd_lat, up, down)


def edge_rows(q, fields, pt, pc):
    return pl.pallas_call(
        rows_kernel,
        out_shape=(jax.ShapeDtypeStruct((ROW_ROWS, COLS), jnp.float32),) * 2,
        in_specs=vmem(4),
        out_specs=tuple(vmem(2)),
        compiler_params=PARAMS,
        name="rows",
    )(q, fields, pt, pc)


def edge_message(tracers, coefs):
    low = (iota(1) & 7) < 4
    return jnp.where(low, coefs, roll(tracers, 4)), jnp.where(low, roll(tracers, -4), coefs)


def tail_block(ref, i):
    lane = iota(1)
    first, second, third = (roll(ref[eight(64 * n + 8 * i), :], 32 * n - USED) for n in range(3))
    return jnp.where(lane < 32, first, jnp.where(lane < 64, second, third))


def halo_tile(a_ref, b_ref, j):
    odd_lat = lax.rem(lax.axis_index("lat"), 2) == 1
    a, b = a_ref[pl.ds(4 * j, 4), :], b_ref[pl.ds(4 * j, 4), :]
    return jnp.concatenate([jnp.where(odd_lat, a, b), jnp.where(odd_lat, b, a)], axis=0)


def strips(pt, pc, mw, me):
    lane = iota(1)
    low = (lane & 7) < 4
    wt = jnp.where(low, roll(mw, -4), pt)
    et = jnp.where(low, pt, roll(me, 4))
    wc = jnp.where(low, mw, pc)
    ec = jnp.where(low, pc, me)
    out = [jnp.where(lane < 48, wt, roll(et, 48))]
    for f in range(4):
        west = jnp.where(lane < 24, roll(wc, -24 * f), roll(wc, 24 - 24 * f))
        east = jnp.where(lane < 72, roll(ec, 48 - 24 * f), roll(ec, 72 - 24 * f))
        out.append(jnp.where(lane < 48, west, east))
    return out


def top_kernel(q_ref, fields, pt_ref, pc_ref, xs_ref, xr_ref, yr_ref, f_ref):
    odd = lax.rem(lax.axis_index("lon"), 2) == 1
    rows = pl.ds(ROWS - 8, 8)
    here = pl.ds(NORTH - 8, 8)
    x, y = tail_block(xr_ref, 7), tail_block(yr_ref, 7)
    mw, me = jnp.where(odd, x, y), jnp.where(odd, y, x)
    tiles = [q_ref[n, here, :] for n in range(6)] + [fields[n, here, :] for n in range(12)]
    tiles += strips(pt_ref[rows, :], pc_ref[rows, :], mw, me)
    f_ref[pl.ds(0, 3), :] = jnp.zeros((3, COLS), jnp.float32)
    for j in range(TILES):
        f_ref[pl.ds(5 * j + 3, 5), :] = tiles[j][3:8, :]
    x, y = xr_ref[pl.ds(BODY + 8, 8), :], yr_ref[pl.ds(BODY + 8, 8), :]
    ew, ee = jnp.where(odd, x, y), jnp.where(odd, y, x)
    f_ref[pl.ds(SEAM, 1), :] = xs_ref[pl.ds(BODY + 12, 1), :]
    f_ref[pl.ds(SEAM + 1, 1), :] = ew[4:5, :]
    f_ref[pl.ds(SEAM + 2, 1), :] = ee[4:5, :]
    f_ref[pl.ds(SEAM + 3, FOLD_ROWS - SEAM - 3), :] = jnp.zeros((FOLD_ROWS - SEAM - 3, COLS), jnp.float32)


def top_rows(q, fields, pt, pc, xs, xr, yr):
    return pl.pallas_call(
        top_kernel,
        out_shape=jax.ShapeDtypeStruct((FOLD_ROWS, COLS), jnp.float32),
        in_specs=vmem(7),
        out_specs=vmem(1)[0],
        compiler_params=PARAMS,
        name="top",
    )(q, fields, pt, pc, xs, xr, yr)


def coefficients(k, s, u, v, kn, ke, ks, kw, sn, se, ss, sw, uw, vs):
    zero = jnp.zeros_like(k)
    fe, fw, fn, fs = 0.5 * (k + ke), 0.5 * (kw + k), 0.5 * (k + kn), 0.5 * (ks + k)
    oe, ow, on, os = s * se, sw * s, s * sn, ss * s
    ae, be = oe * (jnp.maximum(u, zero) + fe), oe * (jnp.minimum(u, zero) - fe)
    aw, bw = ow * (jnp.maximum(uw, zero) + fw), ow * (jnp.minimum(uw, zero) - fw)
    an, bn = on * (jnp.maximum(v, zero) + fn), on * (jnp.minimum(v, zero) - fn)
    a_s, bs = os * (jnp.maximum(vs, zero) + fs), os * (jnp.minimum(vs, zero) - fs)
    centre = s - (ae - bw) - (an - bs)
    return centre, -be, aw, -bn, a_s


def stencil(c, q, e, w, n, s):
    return c[0] * q + c[1] * e + c[2] * w + c[3] * n + c[4] * s


def edges(strip):
    return jnp.where((iota(1) & 7) == 3, strip, roll(strip, -50))


def beside_strip(x, strip, j):
    lane = iota(1)
    west, east = roll(strip, -(8 * j + 3)), roll(strip, -(8 * j + 53))
    return jnp.where(lane == COLS - 1, east, roll(x, -1)), jnp.where(lane == 0, west, roll(x, 1))


def beside(x, edge, j):
    lane = iota(1)
    z = roll(edge, -(8 * j + 3))
    return jnp.where(lane == COLS - 1, z, roll(x, -1)), jnp.where(lane == 0, z, roll(x, 1))


def gather(x, index):
    return jnp.take_along_axis(x, index, axis=1)


def ghost_kernel(p_ref, d_ref, xe_ref, ye_ref, a_ref, b_ref, gy_ref, gx_ref):
    odd = lax.rem(lax.axis_index("lon"), 2) == 1
    row, lane = iota(0), iota(1)
    top = row == 7

    def tile(ref, j):
        return ref[pl.ds(5 * j, 8), :]

    def spread(index_row):
        return jnp.broadcast_to(index_row.astype(jnp.int32) & (COLS - 1), (8, COLS))

    index_d = spread(d_ref[pl.ds(SEAM, 1), :])
    index_p = spread(p_ref[pl.ds(SEAM, 1), :])
    index_pw = spread(p_ref[pl.ds(SEAM + 1, 1), :])
    index_pe = spread(p_ref[pl.ds(SEAM + 2, 1), :])
    xe0, ye0 = xe_ref[pl.ds(BODY, 8), :], ye_ref[pl.ds(BODY, 8), :]
    xe1, ye1 = xe_ref[pl.ds(BODY + 8, 8), :], ye_ref[pl.ds(BODY + 8, 8), :]
    east = [gather(jnp.where(odd, y, x), index_pw) for x, y in ((xe0, ye0), (xe1, ye1))]
    west = [gather(jnp.where(odd, x, y), index_pe) for x, y in ((xe0, ye0), (xe1, ye1))]

    def outer(kind):
        out = jnp.zeros((8, COLS), jnp.float32)
        for j in range(6):
            n = (j, 6 + j % 3, 9 + j % 3)[kind]
            w = jnp.broadcast_to(east[n // 8][n % 8 : n % 8 + 1, :], (8, COLS))
            e = jnp.broadcast_to(west[n // 8][n % 8 : n % 8 + 1, :], (8, COLS))
            out = jnp.where((lane >> 3) == j, roll(w, 8 * j + 4), out)
            out = jnp.where((lane >> 3) == j + 6, roll(e, 8 * j + 52), out)
        return out

    def north(x, ghost):
        return jnp.where(top, ghost, roll(x, -1, 0))

    def below(x):
        return roll(x, 1, 0)

    def field(ref, f, l):
        return tile(ref, 3 * f + l)

    def fold(x, index):
        return roll(gather(x, index), 1, 0)

    def coefs(ref, ghosts, strip_ghosts):
        out = []
        ek, es, eu = (tile(ref, 18 + f) for f in (3, 4, 1))
        for l in range(LEVELS):
            u, v, k, s = (field(ref, f, l) for f in (2, 3, 4, 5))
            ke, kw = beside_strip(k, ek, l)
            se, sw = beside_strip(s, es, l)
            uw = beside_strip(u, eu, l)[1]
            gs, gk = ghosts[l]
            out.append(coefficients(k, s, u, v, north(k, gk), ke, below(k), kw, north(s, gs), se, below(s), sw, uw, below(v)))
        u, v, k, s = (tile(ref, 18 + f) for f in (1, 2, 3, 4))
        gs, gk = strip_ghosts
        out.append(
            coefficients(
                k, s, u, v, north(k, gk), roll(k, -1), below(k), roll(k, 1), north(s, gs), roll(s, -1), below(s), roll(s, 1),
                roll(u, 1), below(v),
            )
        )
        return out

    def advance(c, q, strip, ghosts, strip_ghost):
        out = []
        for j in range(6):
            e, w = beside_strip(q[j], strip, j)
            out.append(stencil(c[j % 3], q[j], e, w, north(q[j], ghosts[j]), below(q[j])))
        new = stencil(c[3], strip, roll(strip, -1), roll(strip, 1), north(strip, strip_ghost), below(strip))
        return out, new

    zero = jnp.zeros((8, COLS), jnp.float32)
    d0 = [tile(d_ref, j) for j in range(6)]
    p0 = [tile(p_ref, j) for j in range(6)]
    static = [(fold(field(d_ref, 5, l), index_p), fold(field(d_ref, 4, l), index_p)) for l in range(LEVELS)]
    cp = coefs(p_ref, static, (outer(1), outer(2)))
    cd = coefs(d_ref, [(zero, zero)] * 3, (zero, zero))
    d1, _ = advance(cd, d0, tile(d_ref, 18), [zero] * 6, zero)
    p1, strip = advance(cp, p0, tile(p_ref, 18), [fold(x, index_p) for x in d0], outer(0))
    p2, strip = advance(cp, p1, strip, [fold(x, index_p) for x in d1], zero)
    p3, _ = advance(cp, p2, strip, [zero] * 6, zero)
    for j in range(6):
        l = j % 3
        values = [p0[j], p1[j], p2[j], p3[j], field(p_ref, 5, l), field(p_ref, 4, l)]
        out = zero
        for i, x in enumerate(values):
            out = jnp.where(row == i, roll(gather(x, index_d), i - 6, 0), out)
        gx_ref[pl.ds(8 * j, 8), :] = out
        gy_ref[pl.ds(8 * j, 8), :] = out
    tracers, coefs = (halo_tile(a_ref, b_ref, PACKED + n) for n in range(2))
    east, west = edge_message(tracers, coefs)
    gx_ref[pl.ds(GHOST_ROWS, 8), :] = jnp.where(odd, west, east)
    gy_ref[pl.ds(GHOST_ROWS, 8), :] = jnp.where(odd, east, west)


def ghosts(partner, own, xr, yr, ar, br):
    return pl.pallas_call(
        ghost_kernel,
        out_shape=(jax.ShapeDtypeStruct((GHOST_ROWS + 8, COLS), jnp.float32),) * 2,
        in_specs=vmem(6),
        out_specs=tuple(vmem(2)),
        compiler_params=PARAMS,
        name="ghost",
    )(partner, own, xr, yr, ar, br)


def coef_block(load, store, beside=beside):
    ku, ks, kk = (load(f, 4, 0) for f in (0, 3, 2))
    for l in range(4):
        u, v, k, s = (load(f, l, 0) for f in range(4))
        if l < 3:
            ke, kw = beside(k, kk, l)
            se, sw = beside(s, ks, l)
            uw = beside(u, ku, l)[1]
        else:
            ke, kw, se, sw, uw = roll(k, -1), roll(k, 1), roll(s, -1), roll(s, 1), roll(u, 1)
        out = coefficients(
            k, s, u, v, load(2, l, 1), ke, load(2, l, -1), kw, load(3, l, 1), se, load(3, l, -1), sw, uw, load(1, l, -1)
        )
        for n in range(5):
            store(n, l, out[n])


def advance(load, c, last, beside=beside):
    edge = load(7, 0)
    out = []
    for j in range(6):
        q = load(j, 0)
        e, w = beside(q, edge, j)
        out.append(stencil([c(n, j % 3) for n in range(5)], q, e, w, load(j, 1), load(j, -1)))
    if not last:
        strip = load(6, 0)
        strip_c = [c(n, 3) for n in range(5)]
        new = stencil(strip_c, strip, roll(strip, -1), roll(strip, 1), load(6, 1), load(6, -1))
        out += [new, edges(new)]
    return out


def outputs(out, sea, store):
    for l in range(LEVELS):
        heat, salt = out[l], out[3 + l]
        dens = sea(l) * (-0.2 * heat * (1.0 + 0.05 * heat) + 0.8 * salt - 0.01 * heat * salt)
        for n, x in enumerate((heat, salt, dens)):
            store(n, l, x)


def eight(r):
    return pl.ds(pl.multiple_of(r, 8), 8)


def coef_kernel(fields, pt_ref, pc_ref, xr_ref, yr_ref, strip_ref, edge_ref, coef):
    odd = lax.rem(lax.axis_index("lon"), 2) == 1

    def put(r, x, y):
        mw, me = jnp.where(odd, x, y), jnp.where(odd, y, x)
        for n, part in enumerate(strips(pt_ref[eight(r), :], pc_ref[eight(r), :], mw, me)):
            strip_ref[n, eight(r + BASE), :] = part
            if n != 2:
                edge_ref[n, eight(r + BASE), :] = edges(part)

    def fill(i, carry):
        put(i * 8, xr_ref[eight(i * 8), :], yr_ref[eight(i * 8), :])
        return carry

    def fill_tail(i, carry):
        put(BODY + i * 8, tail_block(xr_ref, i), tail_block(yr_ref, i))
        return carry

    lax.fori_loop(0, BODY // 8, fill, 0, unroll=UNROLL)
    lax.fori_loop(0, (ROWS - BODY) // 8, fill_tail, 0, unroll=UNROLL)

    def block(i, carry):
        r = i * 8 + BASE

        def load(f, l, shift):
            rows = pl.ds(r + shift, 8)
            if l == 4:
                return edge_ref[1 + f, rows, :]
            return strip_ref[1 + f, rows, :] if l == 3 else fields[3 * f + l, rows, :]

        def store(n, l, x):
            coef[4 * n + l, eight(r), :] = x

        coef_block(load, store)
        return carry

    lax.fori_loop(0, ROWS // 8, block, 0, unroll=UNROLL)


def coefs_of(fields, pt, pc, xr, yr):
    def ext(n):
        return jax.ShapeDtypeStruct((n, EXT, COLS), jnp.float32)

    return pl.pallas_call(
        coef_kernel,
        out_shape=(ext(5), ext(5), ext(20)),
        in_specs=vmem(5),
        out_specs=tuple(vmem(3)),
        compiler_params=PARAMS,
        cost_estimate=pl.CostEstimate(flops=1000, bytes_accessed=1000, transcendentals=0),
        name="coefs",
    )(fields, pt, pc, xr, yr)


def steps_kernel(q_ref, fields, strip_ref, edge_ref, coef, heat_ref, salt_ref, dens_ref, qa, qb, results, sems):
    def loader(src, r):
        def load(j, shift):
            rows = pl.ds(r + shift, 8)
            if src is not None:
                return src[j, rows, :]
            return q_ref[j, rows, :] if j < 6 else (strip_ref, edge_ref)[j - 6][0, rows, :]

        return load

    def coefficient(r):
        return lambda n, l: coef[4 * n + l, eight(r), :]

    def groups(work, start=0, count=GROUPS):
        def body(k, carry):
            later = [work(8 * (GROUP * (k + start) + i) + BASE) for i in range(GROUP)]
            for stores in later:
                for ref, n, rows, x in stores:
                    ref[n, rows, :] = x
            return carry

        lax.fori_loop(0, count, body, 0)

    for src, dst in ((None, qa), (qa, qb), (qb, qa)):

        def block(r):
            return [(dst, j, eight(r), x) for j, x in enumerate(advance(loader(src, r), coefficient(r), False))]

        groups(block)

    def final(r):
        out = []

        def store(n, l, x):
            out.append((results.at[n], l, eight(r - BASE), x))

        outputs(advance(loader(qa, r), coefficient(r), True), lambda l: fields[9 + l, eight(r), :], store)
        return out

    part = ROWS // PARTS
    for p in range(PARTS):
        groups(final, p * GROUPS // PARTS, GROUPS // PARTS)
        rows = pl.ds(p * part, part)
        for n, ref in enumerate((heat_ref, salt_ref, dens_ref)):
            pltpu.make_async_copy(results.at[n, :, rows, :], ref.at[:, rows, :], sems.at[PARTS * n + p]).start()
    for p in range(PARTS):
        rows = pl.ds(p * part, part)
        for n, ref in enumerate((heat_ref, salt_ref, dens_ref)):
            pltpu.make_async_copy(results.at[n, :, rows, :], ref.at[:, rows, :], sems.at[PARTS * n + p]).wait()


def inner_steps(q, fields, strip, edge, coef):
    out = jax.ShapeDtypeStruct((LEVELS, ROWS, COLS), jnp.float32)
    return pl.pallas_call(
        steps_kernel,
        out_shape=(out, out, out),
        in_specs=vmem(5),
        out_specs=(pl.BlockSpec(memory_space=pl.ANY),) * 3,
        scratch_shapes=[
            pltpu.VMEM((8, EXT, COLS), jnp.float32),
            pltpu.VMEM((8, EXT, COLS), jnp.float32),
            pltpu.VMEM((3, LEVELS, ROWS, COLS), jnp.float32),
            pltpu.SemaphoreType.DMA((3 * PARTS,)),
        ],
        compiler_params=PARAMS,
        cost_estimate=pl.CostEstimate(flops=1000, bytes_accessed=1000, transcendentals=0),
        name="steps",
    )(q, fields, strip, edge, coef)


ZONE = 64
SHIFT = NORTH - 48
SOUTH_BLOCKS = (8, 16)
NORTH_BLOCKS = (40, 48)


def zone_kernel(q_ref, fields, strip_ref, a_ref, b_ref, g_ref, gx_ref, gy_ref, *rest):
    h_out, s_out, d_out, *scratch = rest[3:]
    zq, zr, zf, zc, patch, sems = scratch
    odd = lax.rem(lax.axis_index("lon"), 2) == 1
    at_top = lax.axis_index("lat") == LAT - 1
    lane = iota(1)

    def place(j):
        if j < 6:
            return zq, j, q_ref, j
        if j < 18:
            return zf, 4 * ((j - 6) // 3) + j % 3, fields, j - 6
        if j == 18:
            return zq, 6, strip_ref, 0
        return zf, 4 * (j - 19) + 3, strip_ref, j - 18

    x, y = gx_ref[pl.ds(GHOST_ROWS, 8), :], gy_ref[pl.ds(GHOST_ROWS, 8), :]
    packed = [halo_tile(a_ref, b_ref, PACKED + n) for n in range(2)]
    halo = [halo_tile(a_ref, b_ref, j) for j in range(18)]
    halo += strips(*packed, jnp.where(odd, x, y), jnp.where(odd, y, x))
    for j in range(TILES):
        ref, n, src, m = place(j)
        ref[n, pl.ds(BASE, 16), :] = src[m, pl.ds(BASE, 16), :]
        ref[n, pl.ds(32, 16), :] = src[m, pl.ds(NORTH - 16, 16), :]
        ref[n, pl.ds(BASE - 4, 4), :] = halo[j][0:4]
        ref[n, pl.ds(48, 4), :] = halo[j][4:8]

    own = [g_ref[pl.ds(8 * j, 8), :] for j in range(6)]
    strip = jnp.zeros((8, COLS), jnp.float32)
    for j in range(6):
        x, y = gx_ref[pl.ds(8 * j, 8), :], gy_ref[pl.ds(8 * j, 8), :]
        west, east = jnp.where(odd, x, y), jnp.where(odd, y, x)
        strip = jnp.where((lane >> 3) == j, roll(jnp.where(lane >= COLS - 4, west, own[j]), 8 * j + 4), strip)
        strip = jnp.where((lane >> 3) == j + 6, roll(jnp.where(lane < 4, east, own[j]), 8 * j + 52), strip)

    ghost = pl.ds(48, 1)

    def put(ref, s):
        @pl.when(at_top)
        def _():
            for j in range(6):
                ref[j, ghost, :] = own[j][s : s + 1, :]
            ref[6, ghost, :] = strip[s : s + 1, :]

    put(zq, 0)

    @pl.when(at_top)
    def _():
        for f, s in ((3, 4), (2, 5)):
            for l in range(LEVELS):
                zf[4 * f + l, ghost, :] = own[l][s : s + 1, :]
            zf[4 * f + 3, ghost, :] = strip[s : s + 1, :]

    for r in SOUTH_BLOCKS + NORTH_BLOCKS:

        def load(f, l, shift):
            return zf[4 * f + l, pl.ds(r + shift, 8), :]

        def store(n, l, x):
            zc[4 * n + l, pl.ds(r, 8), :] = x

        coef_block(lambda f, l, shift: load(f, min(l, 3), shift), store, beside_strip)

    def loader(src, r):
        def load(j, shift):
            return src[min(j, 6), pl.ds(r + shift, 8), :]

        return load

    def coefficient(r):
        return lambda n, l: zc[4 * n + l, pl.ds(r, 8), :]

    for s, (src, dst) in enumerate(((zq, zr), (zr, zq), (zq, zr))):
        for r in SOUTH_BLOCKS + NORTH_BLOCKS:
            out = advance(loader(src, r), coefficient(r), False, beside_strip)
            for j, x in enumerate(out[:7]):
                dst[j, pl.ds(r, 8), :] = x
        put(dst, s + 1)

    copies = []
    for z, (r, row, part) in enumerate(((16, 0, 0), (40, ROWS - 4, 4))):

        def store(n, l, x):
            patch[2 * n + z, l, :, :] = x

        out = advance(loader(zr, r), coefficient(r), True, beside_strip)
        outputs(out, lambda l: zf[12 + l, pl.ds(r, 8), :], store)
        for n, ref in enumerate((h_out, s_out, d_out)):
            copy = pltpu.make_async_copy(patch.at[2 * n + z, :, pl.ds(part, 4), :], ref.at[:, pl.ds(row, 4), :], sems.at[2 * n + z])
            copy.start()
            copies.append(copy)
    for copy in copies:
        copy.wait()


def zones(q, fields, strip, a, b, g, gx, gy, *results):
    out = jax.ShapeDtypeStruct((LEVELS, ROWS, COLS), jnp.float32)
    anywhere = [pl.BlockSpec(memory_space=pl.ANY)] * 3
    return pl.pallas_call(
        zone_kernel,
        out_shape=(out, out, out),
        in_specs=vmem(8) + anywhere,
        out_specs=tuple(anywhere),
        scratch_shapes=[
            pltpu.VMEM((7, ZONE, COLS), jnp.float32),
            pltpu.VMEM((7, ZONE, COLS), jnp.float32),
            pltpu.VMEM((16, ZONE, COLS), jnp.float32),
            pltpu.VMEM((20, ZONE, COLS), jnp.float32),
            pltpu.VMEM((6, LEVELS, 8, COLS), jnp.float32),
            pltpu.SemaphoreType.DMA((6,)),
        ],
        input_output_aliases={8: 0, 9: 1, 10: 2},
        compiler_params=PARAMS,
        name="zones",
    )(q, fields, strip, a, b, g, gx, gy, *results)


def fold_exchange(message, rotation):
    patterns = [fold_pairs(r) for r in range(LON) if r // HOP % 2 == 0][:-1]
    index = ((rotation >> 4) << 3) + (rotation & 7)
    left_out = index == len(patterns)
    index = jnp.where(left_out, index - HOP, index)
    hops = ((rotation >> 3) & 1) + jnp.where(left_out, 2, 0)
    received = lax.switch(index, [functools.partial(swap, pairs=pairs) for pairs in patterns], message)

    def hop(x, count):
        return swap(x, PAIR_HOP) if count == 0 else hop(swap(x, PAIR_HOP), count - 1)

    return lax.switch(hops, [lambda x: x] + [functools.partial(hop, count=n) for n in range(3)], received)


def on_device(t, s, u, v, k, w, seam):
    m = seam.reshape(1, COLS)
    rotation = ((seam[0] >> 7) + 1 + lax.axis_index("lon")) & (LON - 1)
    ys, xs, pt, pc, q, fields = pack(t, s, u, v, k, w, m)
    a, b = edge_rows(q, fields, pt, pc)
    ar = swap(a, PAIR_A)
    br = swap(b, PAIR_B)
    xr = swap(xs, PAIR_X)
    yr = swap(ys, PAIR_Y)
    message = top_rows(q, fields, pt, pc, xs, xr, yr)
    message, ar, br = lax.optimization_barrier((message, ar, br))
    partner = fold_exchange(message, rotation)
    gy, gx = ghosts(partner, message, xr, yr, ar, br)
    gxr = swap(gx, PAIR_X)
    gyr = swap(gy, PAIR_Y)
    operands, _ = lax.optimization_barrier(((fields, pt, pc, xr, yr), gx))
    strip, edge, coef = coefs_of(*operands)
    results = inner_steps(q, fields, strip, edge, coef)
    return zones(q, fields, strip, ar, br, gx, gxr, gyr, *results)


def solution(mesh):
    block = P(None, "lat", "lon")
    return jax.shard_map(
        on_device,
        mesh=mesh,
        in_specs=(block,) * 6 + (P("lon"),),
        out_specs=(block,) * 3,
        check_vma=False,
    )
```

```python
import functools

import jax
import jax.numpy as jnp
from jax import lax
from jax.experimental import pallas as pl
from jax.experimental.pallas import tpu as pltpu
from jax.sharding import PartitionSpec as P

STEPS = 4
LEVELS = 3
ROWS = 256
COLS = 128
LON = 64
LAT = 4
AXES = ("lon", "lat")
HOP = 8

BASE = 16
NORTH = BASE + ROWS
EXT = 288

TILES = 23
UNROLL = 8
GROUP = 4
GROUPS = ROWS // 8 // GROUP
PARTS = 2

SEAM = 5 * TILES + 3
FOLD_ROWS = 128
PACKED = 18
BODY = 192
USED = 96
ROW_ROWS = 4 * 20
GHOST_ROWS = 48


def flat(lon, lat):
    return (lon % LON) * LAT + lat


def lon_pairs(partner):
    return [(flat(i, a), flat(partner(i), a)) for i in range(LON) for a in range(LAT)]


PAIR_X = lon_pairs(lambda i: i ^ 1)
PAIR_Y = lon_pairs(lambda i: ((i - 1) ^ 1) + 1)
PAIR_A = [(flat(i, a), flat(i, a ^ 1)) for i in range(LON) for a in range(LAT)]
PAIR_B = [(flat(i, a), flat(i, 3 - a)) for i in range(LON) for a in (1, 2)]


PAIR_HOP = [(flat(i, LAT - 1), flat(i + HOP, LAT - 1)) for i in range(LON)]


def fold_pairs(r):
    return [(flat(i, LAT - 1), flat(r - 1 - i, LAT - 1)) for i in range(LON)]


def swap(x, pairs):
    return lax.ppermute(x, AXES, pairs)


def iota(axis):
    return lax.broadcasted_iota(jnp.int32, (8, COLS), axis)


def roll(x, shift, axis=1):
    return pltpu.roll(x, shift % x.shape[axis], axis)


def sea_of(x):
    return x.astype(jnp.float32)


def vmem(n):
    return [pl.BlockSpec(memory_space=pltpu.VMEM)] * n


PARAMS = pltpu.CompilerParams(vmem_limit_bytes=32 << 20)


def pack_kernel(t_hbm, s_hbm, u_hbm, v_hbm, k_hbm, w_hbm, m_hbm, ys_ref, xs_ref, pt_ref, pc_ref, q_ref, f_ref, w_ref, m_ref, tail_ref, sems):
    odd = lax.rem(lax.axis_index("lon"), 2) == 1
    lane = iota(1)
    group = lane >> 3
    own = pl.ds(BASE, ROWS)

    def target(n):
        if n >= 5:
            return (w_ref, m_ref)[n - 5]
        ref = q_ref if n < 2 else f_ref
        return ref.at[pl.ds(3 * (n if n < 2 else n - 2), LEVELS), own, :]

    copies = [
        pltpu.make_async_copy(src, target(n), sems.at[n])
        for n, src in enumerate((t_hbm, s_hbm, u_hbm, v_hbm, k_hbm, w_hbm, m_hbm))
    ]
    for copy in copies:
        copy.start()

    def gathered(ref, count, rows):
        out = jnp.zeros((8, COLS), jnp.float32)
        for j in range(count):
            out = jnp.where(group == j, roll(ref[j, rows, :], 4 + 8 * j), out)
        return out

    def tracer_block(i, carry):
        rows = pl.ds(pl.multiple_of(i * 8 + BASE, 8), 8)
        pt_ref[pl.ds(pl.multiple_of(i * 8, 8), 8), :] = gathered(q_ref, 6, rows)
        return carry

    def messages(i):
        rows = eight(i * 8)
        here = eight(i * 8 + BASE)
        for l in range(LEVELS):
            f_ref[9 + l, here, :] = sea_of(w_ref[l, rows, :])
        tracers = pt_ref[rows, :]
        coefs = gathered(f_ref, 12, here)
        pc_ref[rows, :] = coefs
        east, west = edge_message(tracers, coefs)
        return jnp.where(odd, west, east), jnp.where(odd, east, west)

    def last_block(i, carry):
        for n, x in enumerate(messages(i + BODY // 8)):
            tail_ref[n, eight(i * 8), :] = x
        return carry

    def coef_block(third):
        def block(i, carry):
            for n, (ref, x) in enumerate(zip((xs_ref, ys_ref), messages(8 * third + i))):
                rest = roll(tail_ref[n, eight(i * 8), :], USED - 32 * third)
                ref[eight(64 * third + i * 8), :] = jnp.where(lane < USED, x, rest)
            return carry

        return block

    copies[0].wait()
    copies[1].wait()
    lax.fori_loop(0, ROWS // 8, tracer_block, 0, unroll=8)
    for copy in copies[2:]:
        copy.wait()
    lax.fori_loop(0, 8, last_block, 0, unroll=UNROLL)
    for third in range(3):
        lax.fori_loop(0, 8, coef_block(third), 0, unroll=UNROLL)
    second = pl.ds(BASE + ROWS - 2, 1)
    for out in (xs_ref, ys_ref):
        for n in range(6):
            out[pl.ds(BODY + n, 1), :] = q_ref[n, second, :]
        for l in range(LEVELS):
            out[pl.ds(BODY + 6 + l, 1), :] = f_ref[9 + l, second, :]
            out[pl.ds(BODY + 9 + l, 1), :] = f_ref[6 + l, second, :]
        out[pl.ds(BODY + 12, 1), :] = m_ref[...].astype(jnp.float32)
        out[pl.ds(BODY + 13, 3), :] = jnp.zeros((3, COLS), jnp.float32)


def pack(t, s, u, v, k, w, m):
    edge = jax.ShapeDtypeStruct((BODY + 16, COLS), jnp.float32)
    own = jax.ShapeDtypeStruct((ROWS, COLS), jnp.float32)
    return pl.pallas_call(
        pack_kernel,
        out_shape=(
            edge,
            edge,
            own,
            own,
            jax.ShapeDtypeStruct((6, EXT, COLS), jnp.float32),
            jax.ShapeDtypeStruct((12, EXT, COLS), jnp.float32),
        ),
        in_specs=[pl.BlockSpec(memory_space=pltpu.HBM)] * 7,
        out_specs=tuple(vmem(6)),
        scratch_shapes=[
            pltpu.VMEM((LEVELS, ROWS, COLS), jnp.int32),
            pltpu.VMEM((1, COLS), jnp.int32),
            pltpu.VMEM((2, ROWS - BODY, COLS), jnp.float32),
            pltpu.SemaphoreType.DMA((7,)),
        ],
        compiler_params=PARAMS,
        name="pack",
    )(*(pltpu.with_memory_space_constraint(x, pltpu.HBM) for x in (t, s, u, v, k, w, m)))


def rows_kernel(q_ref, fields, pt_ref, pc_ref, a_ref, b_ref):
    odd_lat = lax.rem(lax.axis_index("lat"), 2) == 1
    for j in range(20):
        if j < 18:
            ref, n = (q_ref, j) if j < 6 else (fields, j - 6)
            down, up = ref[n, pl.ds(BASE, 8), :][0:4], ref[n, pl.ds(NORTH - 8, 8), :][4:8]
        else:
            ref = (pt_ref, pc_ref)[j - 18]
            down, up = ref[pl.ds(0, 8), :][0:4], ref[pl.ds(ROWS - 8, 8), :][4:8]
        a_ref[pl.ds(4 * j, 4), :] = jnp.where(odd_lat, down, up)
        b_ref[pl.ds(4 * j, 4), :] = jnp.where(odd_lat, up, down)


def edge_rows(q, fields, pt, pc):
    return pl.pallas_call(
        rows_kernel,
        out_shape=(jax.ShapeDtypeStruct((ROW_ROWS, COLS), jnp.float32),) * 2,
        in_specs=vmem(4),
        out_specs=tuple(vmem(2)),
        compiler_params=PARAMS,
        name="rows",
    )(q, fields, pt, pc)


def edge_message(tracers, coefs):
    low = (iota(1) & 7) < 4
    return jnp.where(low, coefs, roll(tracers, 4)), jnp.where(low, roll(tracers, -4), coefs)


def tail_block(ref, i):
    lane = iota(1)
    first, second, third = (roll(ref[eight(64 * n + 8 * i), :], 32 * n - USED) for n in range(3))
    return jnp.where(lane < 32, first, jnp.where(lane < 64, second, third))


def halo_tile(a_ref, b_ref, j):
    odd_lat = lax.rem(lax.axis_index("lat"), 2) == 1
    a, b = a_ref[pl.ds(4 * j, 4), :], b_ref[pl.ds(4 * j, 4), :]
    return jnp.concatenate([jnp.where(odd_lat, a, b), jnp.where(odd_lat, b, a)], axis=0)


def strips(pt, pc, mw, me):
    lane = iota(1)
    low = (lane & 7) < 4
    wt = jnp.where(low, roll(mw, -4), pt)
    et = jnp.where(low, pt, roll(me, 4))
    wc = jnp.where(low, mw, pc)
    ec = jnp.where(low, pc, me)
    out = [jnp.where(lane < 48, wt, roll(et, 48))]
    for f in range(4):
        west = jnp.where(lane < 24, roll(wc, -24 * f), roll(wc, 24 - 24 * f))
        east = jnp.where(lane < 72, roll(ec, 48 - 24 * f), roll(ec, 72 - 24 * f))
        out.append(jnp.where(lane < 48, west, east))
    return out


def top_kernel(q_ref, fields, pt_ref, pc_ref, xs_ref, xr_ref, yr_ref, f_ref):
    odd = lax.rem(lax.axis_index("lon"), 2) == 1
    rows = pl.ds(ROWS - 8, 8)
    here = pl.ds(NORTH - 8, 8)
    x, y = tail_block(xr_ref, 7), tail_block(yr_ref, 7)
    mw, me = jnp.where(odd, x, y), jnp.where(odd, y, x)
    tiles = [q_ref[n, here, :] for n in range(6)] + [fields[n, here, :] for n in range(12)]
    tiles += strips(pt_ref[rows, :], pc_ref[rows, :], mw, me)
    f_ref[pl.ds(0, 3), :] = jnp.zeros((3, COLS), jnp.float32)
    for j in range(TILES):
        f_ref[pl.ds(5 * j + 3, 5), :] = tiles[j][3:8, :]
    x, y = xr_ref[pl.ds(BODY + 8, 8), :], yr_ref[pl.ds(BODY + 8, 8), :]
    ew, ee = jnp.where(odd, x, y), jnp.where(odd, y, x)
    f_ref[pl.ds(SEAM, 1), :] = xs_ref[pl.ds(BODY + 12, 1), :]
    f_ref[pl.ds(SEAM + 1, 1), :] = ew[4:5, :]
    f_ref[pl.ds(SEAM + 2, 1), :] = ee[4:5, :]
    f_ref[pl.ds(SEAM + 3, FOLD_ROWS - SEAM - 3), :] = jnp.zeros((FOLD_ROWS - SEAM - 3, COLS), jnp.float32)


def top_rows(q, fields, pt, pc, xs, xr, yr):
    return pl.pallas_call(
        top_kernel,
        out_shape=jax.ShapeDtypeStruct((FOLD_ROWS, COLS), jnp.float32),
        in_specs=vmem(7),
        out_specs=vmem(1)[0],
        compiler_params=PARAMS,
        name="top",
    )(q, fields, pt, pc, xs, xr, yr)


def coefficients(k, s, u, v, kn, ke, ks, kw, sn, se, ss, sw, uw, vs):
    zero = jnp.zeros_like(k)
    fe, fw, fn, fs = 0.5 * (k + ke), 0.5 * (kw + k), 0.5 * (k + kn), 0.5 * (ks + k)
    oe, ow, on, os = s * se, sw * s, s * sn, ss * s
    ae, be = oe * (jnp.maximum(u, zero) + fe), oe * (jnp.minimum(u, zero) - fe)
    aw, bw = ow * (jnp.maximum(uw, zero) + fw), ow * (jnp.minimum(uw, zero) - fw)
    an, bn = on * (jnp.maximum(v, zero) + fn), on * (jnp.minimum(v, zero) - fn)
    a_s, bs = os * (jnp.maximum(vs, zero) + fs), os * (jnp.minimum(vs, zero) - fs)
    centre = s - (ae - bw) - (an - bs)
    return centre, -be, aw, -bn, a_s


def stencil(c, q, e, w, n, s):
    return c[0] * q + c[1] * e + c[2] * w + c[3] * n + c[4] * s


def edges(strip):
    return jnp.where((iota(1) & 7) == 3, strip, roll(strip, -50))


def beside_strip(x, strip, j):
    lane = iota(1)
    west, east = roll(strip, -(8 * j + 3)), roll(strip, -(8 * j + 53))
    return jnp.where(lane == COLS - 1, east, roll(x, -1)), jnp.where(lane == 0, west, roll(x, 1))


def beside(x, edge, j):
    lane = iota(1)
    z = roll(edge, -(8 * j + 3))
    return jnp.where(lane == COLS - 1, z, roll(x, -1)), jnp.where(lane == 0, z, roll(x, 1))


def gather(x, index):
    return jnp.take_along_axis(x, index, axis=1)


def ghost_kernel(p_ref, d_ref, xe_ref, ye_ref, a_ref, b_ref, gy_ref, gx_ref):
    odd = lax.rem(lax.axis_index("lon"), 2) == 1
    row, lane = iota(0), iota(1)
    top = row == 7

    def tile(ref, j):
        return ref[pl.ds(5 * j, 8), :]

    def spread(index_row):
        return jnp.broadcast_to(index_row.astype(jnp.int32) & (COLS - 1), (8, COLS))

    index_d = spread(d_ref[pl.ds(SEAM, 1), :])
    index_p = spread(p_ref[pl.ds(SEAM, 1), :])
    index_pw = spread(p_ref[pl.ds(SEAM + 1, 1), :])
    index_pe = spread(p_ref[pl.ds(SEAM + 2, 1), :])
    xe0, ye0 = xe_ref[pl.ds(BODY, 8), :], ye_ref[pl.ds(BODY, 8), :]
    xe1, ye1 = xe_ref[pl.ds(BODY + 8, 8), :], ye_ref[pl.ds(BODY + 8, 8), :]
    east = [gather(jnp.where(odd, y, x), index_pw) for x, y in ((xe0, ye0), (xe1, ye1))]
    west = [gather(jnp.where(odd, x, y), index_pe) for x, y in ((xe0, ye0), (xe1, ye1))]

    def outer(kind):
        out = jnp.zeros((8, COLS), jnp.float32)
        for j in range(6):
            n = (j, 6 + j % 3, 9 + j % 3)[kind]
            w = jnp.broadcast_to(east[n // 8][n % 8 : n % 8 + 1, :], (8, COLS))
            e = jnp.broadcast_to(west[n // 8][n % 8 : n % 8 + 1, :], (8, COLS))
            out = jnp.where((lane >> 3) == j, roll(w, 8 * j + 4), out)
            out = jnp.where((lane >> 3) == j + 6, roll(e, 8 * j + 52), out)
        return out

    def north(x, ghost):
        return jnp.where(top, ghost, roll(x, -1, 0))

    def below(x):
        return roll(x, 1, 0)

    def field(ref, f, l):
        return tile(ref, 3 * f + l)

    def fold(x, index):
        return roll(gather(x, index), 1, 0)

    def coefs(ref, ghosts, strip_ghosts):
        out = []
        ek, es, eu = (tile(ref, 18 + f) for f in (3, 4, 1))
        for l in range(LEVELS):
            u, v, k, s = (field(ref, f, l) for f in (2, 3, 4, 5))
            ke, kw = beside_strip(k, ek, l)
            se, sw = beside_strip(s, es, l)
            uw = beside_strip(u, eu, l)[1]
            gs, gk = ghosts[l]
            out.append(coefficients(k, s, u, v, north(k, gk), ke, below(k), kw, north(s, gs), se, below(s), sw, uw, below(v)))
        u, v, k, s = (tile(ref, 18 + f) for f in (1, 2, 3, 4))
        gs, gk = strip_ghosts
        out.append(
            coefficients(
                k, s, u, v, north(k, gk), roll(k, -1), below(k), roll(k, 1), north(s, gs), roll(s, -1), below(s), roll(s, 1),
                roll(u, 1), below(v),
            )
        )
        return out

    def advance(c, q, strip, ghosts, strip_ghost):
        out = []
        for j in range(6):
            e, w = beside_strip(q[j], strip, j)
            out.append(stencil(c[j % 3], q[j], e, w, north(q[j], ghosts[j]), below(q[j])))
        new = stencil(c[3], strip, roll(strip, -1), roll(strip, 1), north(strip, strip_ghost), below(strip))
        return out, new

    zero = jnp.zeros((8, COLS), jnp.float32)
    d0 = [tile(d_ref, j) for j in range(6)]
    p0 = [tile(p_ref, j) for j in range(6)]
    static = [(fold(field(d_ref, 5, l), index_p), fold(field(d_ref, 4, l), index_p)) for l in range(LEVELS)]
    cp = coefs(p_ref, static, (outer(1), outer(2)))
    cd = coefs(d_ref, [(zero, zero)] * 3, (zero, zero))
    d1, _ = advance(cd, d0, tile(d_ref, 18), [zero] * 6, zero)
    p1, strip = advance(cp, p0, tile(p_ref, 18), [fold(x, index_p) for x in d0], outer(0))
    p2, strip = advance(cp, p1, strip, [fold(x, index_p) for x in d1], zero)
    p3, _ = advance(cp, p2, strip, [zero] * 6, zero)
    for j in range(6):
        l = j % 3
        values = [p0[j], p1[j], p2[j], p3[j], field(p_ref, 5, l), field(p_ref, 4, l)]
        out = zero
        for i, x in enumerate(values):
            out = jnp.where(row == i, roll(gather(x, index_d), i - 6, 0), out)
        gx_ref[pl.ds(8 * j, 8), :] = out
        gy_ref[pl.ds(8 * j, 8), :] = out
    tracers, coefs = (halo_tile(a_ref, b_ref, PACKED + n) for n in range(2))
    east, west = edge_message(tracers, coefs)
    gx_ref[pl.ds(GHOST_ROWS, 8), :] = jnp.where(odd, west, east)
    gy_ref[pl.ds(GHOST_ROWS, 8), :] = jnp.where(odd, east, west)


def ghosts(partner, own, xr, yr, ar, br):
    return pl.pallas_call(
        ghost_kernel,
        out_shape=(jax.ShapeDtypeStruct((GHOST_ROWS + 8, COLS), jnp.float32),) * 2,
        in_specs=vmem(6),
        out_specs=tuple(vmem(2)),
        compiler_params=PARAMS,
        name="ghost",
    )(partner, own, xr, yr, ar, br)


def coef_block(load, store, beside=beside):
    ku, ks, kk = (load(f, 4, 0) for f in (0, 3, 2))
    for l in range(4):
        u, v, k, s = (load(f, l, 0) for f in range(4))
        if l < 3:
            ke, kw = beside(k, kk, l)
            se, sw = beside(s, ks, l)
            uw = beside(u, ku, l)[1]
        else:
            ke, kw, se, sw, uw = roll(k, -1), roll(k, 1), roll(s, -1), roll(s, 1), roll(u, 1)
        out = coefficients(
            k, s, u, v, load(2, l, 1), ke, load(2, l, -1), kw, load(3, l, 1), se, load(3, l, -1), sw, uw, load(1, l, -1)
        )
        for n in range(5):
            store(n, l, out[n])


def advance(load, c, last, beside=beside):
    edge = load(7, 0)
    out = []
    for j in range(6):
        q = load(j, 0)
        e, w = beside(q, edge, j)
        out.append(stencil([c(n, j % 3) for n in range(5)], q, e, w, load(j, 1), load(j, -1)))
    if not last:
        strip = load(6, 0)
        strip_c = [c(n, 3) for n in range(5)]
        new = stencil(strip_c, strip, roll(strip, -1), roll(strip, 1), load(6, 1), load(6, -1))
        out += [new, edges(new)]
    return out


def outputs(out, sea, store):
    for l in range(LEVELS):
        heat, salt = out[l], out[3 + l]
        dens = sea(l) * (-0.2 * heat * (1.0 + 0.05 * heat) + 0.8 * salt - 0.01 * heat * salt)
        for n, x in enumerate((heat, salt, dens)):
            store(n, l, x)


def eight(r):
    return pl.ds(pl.multiple_of(r, 8), 8)


def coef_kernel(fields, pt_ref, pc_ref, xr_ref, yr_ref, strip_ref, edge_ref, coef):
    odd = lax.rem(lax.axis_index("lon"), 2) == 1

    def put(r, x, y):
        mw, me = jnp.where(odd, x, y), jnp.where(odd, y, x)
        for n, part in enumerate(strips(pt_ref[eight(r), :], pc_ref[eight(r), :], mw, me)):
            strip_ref[n, eight(r + BASE), :] = part
            if n != 2:
                edge_ref[n, eight(r + BASE), :] = edges(part)

    def fill(i, carry):
        put(i * 8, xr_ref[eight(i * 8), :], yr_ref[eight(i * 8), :])
        return carry

    def fill_tail(i, carry):
        put(BODY + i * 8, tail_block(xr_ref, i), tail_block(yr_ref, i))
        return carry

    lax.fori_loop(0, BODY // 8, fill, 0, unroll=UNROLL)
    lax.fori_loop(0, (ROWS - BODY) // 8, fill_tail, 0, unroll=UNROLL)

    def block(i, carry):
        r = i * 8 + BASE

        def load(f, l, shift):
            rows = pl.ds(r + shift, 8)
            if l == 4:
                return edge_ref[1 + f, rows, :]
            return strip_ref[1 + f, rows, :] if l == 3 else fields[3 * f + l, rows, :]

        def store(n, l, x):
            coef[4 * n + l, eight(r), :] = x

        coef_block(load, store)
        return carry

    lax.fori_loop(0, ROWS // 8, block, 0, unroll=UNROLL)


def coefs_of(fields, pt, pc, xr, yr):
    def ext(n):
        return jax.ShapeDtypeStruct((n, EXT, COLS), jnp.float32)

    return pl.pallas_call(
        coef_kernel,
        out_shape=(ext(5), ext(5), ext(20)),
        in_specs=vmem(5),
        out_specs=tuple(vmem(3)),
        compiler_params=PARAMS,
        cost_estimate=pl.CostEstimate(flops=1000, bytes_accessed=1000, transcendentals=0),
        name="coefs",
    )(fields, pt, pc, xr, yr)


def steps_kernel(q_ref, fields, strip_ref, edge_ref, coef, heat_ref, salt_ref, dens_ref, qa, qb, results, sems):
    def loader(src, r):
        def load(j, shift):
            rows = pl.ds(r + shift, 8)
            if src is not None:
                return src[j, rows, :]
            return q_ref[j, rows, :] if j < 6 else (strip_ref, edge_ref)[j - 6][0, rows, :]

        return load

    def coefficient(r):
        return lambda n, l: coef[4 * n + l, eight(r), :]

    def groups(work, start=0, count=GROUPS):
        def body(k, carry):
            later = [work(8 * (GROUP * (k + start) + i) + BASE) for i in range(GROUP)]
            for stores in later:
                for ref, n, rows, x in stores:
                    ref[n, rows, :] = x
            return carry

        lax.fori_loop(0, count, body, 0)

    for src, dst in ((None, qa), (qa, qb), (qb, qa)):

        def block(r):
            return [(dst, j, eight(r), x) for j, x in enumerate(advance(loader(src, r), coefficient(r), False))]

        groups(block)

    def final(r):
        out = []

        def store(n, l, x):
            out.append((results.at[n], l, eight(r - BASE), x))

        outputs(advance(loader(qa, r), coefficient(r), True), lambda l: fields[9 + l, eight(r), :], store)
        return out

    part = ROWS // PARTS
    for p in range(PARTS):
        groups(final, p * GROUPS // PARTS, GROUPS // PARTS)
        rows = pl.ds(p * part, part)
        for n, ref in enumerate((heat_ref, salt_ref, dens_ref)):
            pltpu.make_async_copy(results.at[n, :, rows, :], ref.at[:, rows, :], sems.at[PARTS * n + p]).start()
    for p in range(PARTS):
        rows = pl.ds(p * part, part)
        for n, ref in enumerate((heat_ref, salt_ref, dens_ref)):
            pltpu.make_async_copy(results.at[n, :, rows, :], ref.at[:, rows, :], sems.at[PARTS * n + p]).wait()


def inner_steps(q, fields, strip, edge, coef):
    out = jax.ShapeDtypeStruct((LEVELS, ROWS, COLS), jnp.float32)
    return pl.pallas_call(
        steps_kernel,
        out_shape=(out, out, out),
        in_specs=vmem(5),
        out_specs=(pl.BlockSpec(memory_space=pl.ANY),) * 3,
        scratch_shapes=[
            pltpu.VMEM((8, EXT, COLS), jnp.float32),
            pltpu.VMEM((8, EXT, COLS), jnp.float32),
            pltpu.VMEM((3, LEVELS, ROWS, COLS), jnp.float32),
            pltpu.SemaphoreType.DMA((3 * PARTS,)),
        ],
        compiler_params=PARAMS,
        cost_estimate=pl.CostEstimate(flops=1000, bytes_accessed=1000, transcendentals=0),
        name="steps",
    )(q, fields, strip, edge, coef)


ZONE = 64
SHIFT = NORTH - 48
SOUTH_BLOCKS = (8, 16)
NORTH_BLOCKS = (40, 48)


def zone_kernel(q_ref, fields, strip_ref, a_ref, b_ref, g_ref, gx_ref, gy_ref, *rest):
    h_out, s_out, d_out, *scratch = rest[3:]
    zq, zr, zf, zc, patch, sems = scratch
    odd = lax.rem(lax.axis_index("lon"), 2) == 1
    at_top = lax.axis_index("lat") == LAT - 1
    lane = iota(1)

    def place(j):
        if j < 6:
            return zq, j, q_ref, j
        if j < 18:
            return zf, 4 * ((j - 6) // 3) + j % 3, fields, j - 6
        if j == 18:
            return zq, 6, strip_ref, 0
        return zf, 4 * (j - 19) + 3, strip_ref, j - 18

    x, y = gx_ref[pl.ds(GHOST_ROWS, 8), :], gy_ref[pl.ds(GHOST_ROWS, 8), :]
    packed = [halo_tile(a_ref, b_ref, PACKED + n) for n in range(2)]
    halo = [halo_tile(a_ref, b_ref, j) for j in range(18)]
    halo += strips(*packed, jnp.where(odd, x, y), jnp.where(odd, y, x))
    for j in range(TILES):
        ref, n, src, m = place(j)
        ref[n, pl.ds(BASE, 16), :] = src[m, pl.ds(BASE, 16), :]
        ref[n, pl.ds(32, 16), :] = src[m, pl.ds(NORTH - 16, 16), :]
        ref[n, pl.ds(BASE - 4, 4), :] = halo[j][0:4]
        ref[n, pl.ds(48, 4), :] = halo[j][4:8]

    own = [g_ref[pl.ds(8 * j, 8), :] for j in range(6)]
    strip = jnp.zeros((8, COLS), jnp.float32)
    for j in range(6):
        x, y = gx_ref[pl.ds(8 * j, 8), :], gy_ref[pl.ds(8 * j, 8), :]
        west, east = jnp.where(odd, x, y), jnp.where(odd, y, x)
        strip = jnp.where((lane >> 3) == j, roll(jnp.where(lane >= COLS - 4, west, own[j]), 8 * j + 4), strip)
        strip = jnp.where((lane >> 3) == j + 6, roll(jnp.where(lane < 4, east, own[j]), 8 * j + 52), strip)

    ghost = pl.ds(48, 1)

    def put(ref, s):
        @pl.when(at_top)
        def _():
            for j in range(6):
                ref[j, ghost, :] = own[j][s : s + 1, :]
            ref[6, ghost, :] = strip[s : s + 1, :]

    put(zq, 0)

    @pl.when(at_top)
    def _():
        for f, s in ((3, 4), (2, 5)):
            for l in range(LEVELS):
                zf[4 * f + l, ghost, :] = own[l][s : s + 1, :]
            zf[4 * f + 3, ghost, :] = strip[s : s + 1, :]

    for r in SOUTH_BLOCKS + NORTH_BLOCKS:

        def load(f, l, shift):
            return zf[4 * f + l, pl.ds(r + shift, 8), :]

        def store(n, l, x):
            zc[4 * n + l, pl.ds(r, 8), :] = x

        coef_block(lambda f, l, shift: load(f, min(l, 3), shift), store, beside_strip)

    def loader(src, r):
        def load(j, shift):
            return src[min(j, 6), pl.ds(r + shift, 8), :]

        return load

    def coefficient(r):
        return lambda n, l: zc[4 * n + l, pl.ds(r, 8), :]

    for s, (src, dst) in enumerate(((zq, zr), (zr, zq), (zq, zr))):
        for r in SOUTH_BLOCKS + NORTH_BLOCKS:
            out = advance(loader(src, r), coefficient(r), False, beside_strip)
            for j, x in enumerate(out[:7]):
                dst[j, pl.ds(r, 8), :] = x
        put(dst, s + 1)

    copies = []
    for z, (r, row, part) in enumerate(((16, 0, 0), (40, ROWS - 4, 4))):

        def store(n, l, x):
            patch[2 * n + z, l, :, :] = x

        out = advance(loader(zr, r), coefficient(r), True, beside_strip)
        outputs(out, lambda l: zf[12 + l, pl.ds(r, 8), :], store)
        for n, ref in enumerate((h_out, s_out, d_out)):
            copy = pltpu.make_async_copy(patch.at[2 * n + z, :, pl.ds(part, 4), :], ref.at[:, pl.ds(row, 4), :], sems.at[2 * n + z])
            copy.start()
            copies.append(copy)
    for copy in copies:
        copy.wait()


def zones(q, fields, strip, a, b, g, gx, gy, *results):
    out = jax.ShapeDtypeStruct((LEVELS, ROWS, COLS), jnp.float32)
    anywhere = [pl.BlockSpec(memory_space=pl.ANY)] * 3
    return pl.pallas_call(
        zone_kernel,
        out_shape=(out, out, out),
        in_specs=vmem(8) + anywhere,
        out_specs=tuple(anywhere),
        scratch_shapes=[
            pltpu.VMEM((7, ZONE, COLS), jnp.float32),
            pltpu.VMEM((7, ZONE, COLS), jnp.float32),
            pltpu.VMEM((16, ZONE, COLS), jnp.float32),
            pltpu.VMEM((20, ZONE, COLS), jnp.float32),
            pltpu.VMEM((6, LEVELS, 8, COLS), jnp.float32),
            pltpu.SemaphoreType.DMA((6,)),
        ],
        input_output_aliases={8: 0, 9: 1, 10: 2},
        compiler_params=PARAMS,
        name="zones",
    )(q, fields, strip, a, b, g, gx, gy, *results)


def fold_exchange(message, rotation):
    patterns = [fold_pairs(r) for r in range(LON) if r // HOP % 2 == 0][:-1]
    index = ((rotation >> 4) << 3) + (rotation & 7)
    left_out = index == len(patterns)
    index = jnp.where(left_out, index - HOP, index)
    hops = ((rotation >> 3) & 1) + jnp.where(left_out, 2, 0)
    received = lax.switch(index, [functools.partial(swap, pairs=pairs) for pairs in patterns], message)

    def hop(x, count):
        return swap(x, PAIR_HOP) if count == 0 else hop(swap(x, PAIR_HOP), count - 1)

    return lax.switch(hops, [lambda x: x] + [functools.partial(hop, count=n) for n in range(3)], received)


def on_device(t, s, u, v, k, w, seam):
    m = seam.reshape(1, COLS)
    rotation = ((seam[0] >> 7) + 1 + lax.axis_index("lon")) & (LON - 1)
    ys, xs, pt, pc, q, fields = pack(t, s, u, v, k, w, m)
    a, b = edge_rows(q, fields, pt, pc)
    xs, a, b = lax.optimization_barrier((xs, a, b))
    ar = swap(a, PAIR_A)
    br = swap(b, PAIR_B)
    xr = swap(xs, PAIR_X)
    yr = swap(ys, PAIR_Y)
    message = top_rows(q, fields, pt, pc, xs, xr, yr)
    message, ar, br = lax.optimization_barrier((message, ar, br))
    partner = fold_exchange(message, rotation)
    gy, gx = ghosts(partner, message, xr, yr, ar, br)
    gxr = swap(gx, PAIR_X)
    gyr = swap(gy, PAIR_Y)
    operands, _ = lax.optimization_barrier(((fields, pt, pc, xr, yr), gx))
    strip, edge, coef = coefs_of(*operands)
    results = inner_steps(q, fields, strip, edge, coef)
    return zones(q, fields, strip, ar, br, gx, gxr, gyr, *results)


def solution(mesh):
    block = P(None, "lat", "lon")
    return jax.shard_map(
        on_device,
        mesh=mesh,
        in_specs=(block,) * 6 + (P("lon"),),
        out_specs=(block,) * 3,
        check_vma=False,
    )
```
